128 devices in a mesh: dp: 2 (over core), seq: 16 (over x, z), head: 4 (over y).
Axes of the slice: x: 4, y: 4, z: 4, core: 2. Of those that a mesh axis runs over, the one named last changes fastest.
Arguments:
- hidden: bfloat16 [2, 8192, 1536], P('dp', 'seq'), may hold values from -6 to 6
- cotangent: bfloat16 [2, 8192, 1536], P('dp', 'seq'), may hold values from -6 to 6
- norm_gain: float32 [1536], replicated, may hold values from 0.1 to 1.9
- w_z: bfloat16 [1536, 3072], P(None, 'head'), may hold values from -0.15625 to 0.15625
- w_x: bfloat16 [1536, 3072], P(None, 'head'), may hold values from -0.15625 to 0.15625
- w_bc: bfloat16 [1536, 256], replicated, may hold values from -0.15625 to 0.15625
- w_dt: bfloat16 [1536, 48], P(None, 'head'), may hold values from -0.3125 to 0.3125
- conv_x: float32 [4, 3072], P(None, 'head'), may hold values from -3 to 3
- conv_bc: float32 [4, 256], replicated, may hold values from -3 to 3
- bias_x: float32 [3072], P('head'), may hold values from -3 to 3
- bias_bc: float32 [256], replicated, may hold values from -3 to 3
- dt_bias: float32 [48], P('head'), may hold values from -6.5 to -4.5
- a_log: float32 [48], P('head'), may hold values from -4.6 to 0.7
- skip_d: float32 [48], P('head'), may hold values from 0.5 to 1.5
- gain_out: float32 [3072], P('head'), may hold values from 0.1 to 1.9
- w_out: bfloat16 [3072, 1536], P('head'), may hold values from -0.109375 to 0.109375
Outputs:
- output: bfloat16 [2, 8192, 1536], P('dp', 'seq', 'head')
- hidden_grad: bfloat16 [2, 8192, 1536], P('dp', 'seq', 'head')
- grad_norm_gain: float32 [1536], P('head')
- grad_w_z: float32 [1536, 3072], P(None, 'head')
- grad_w_x: float32 [1536, 3072], P(None, 'head')
- grad_w_bc: float32 [1536, 256], P(None, 'head')
- grad_w_dt: float32 [1536, 48], P(None, 'head')
- grad_conv_x: float32 [4, 3072], P(None, 'head')
- grad_conv_bc: float32 [4, 256], replicated
- grad_bias_x: float32 [3072], P('head')
- grad_bias_bc: float32 [256], replicated
- grad_dt_bias: float32 [48], P('head')
- grad_a_log: float32 [48], P('head')
- grad_skip_d: float32 [48], P('head')
- grad_gain_out: float32 [3072], P('head')
- grad_w_out: float32 [3072, 1536], P('head')
The draws below stay inside these ranges and needn't reach their ends.
All inputs are finite; a program needn't handle non-finite values.
Results may differ from the reference program's by a relative error of at most 0.012.
The reference program's roundings to bfloat16 on the way count: a program that leaves them out, or rounds other values in their place, can miss the bound.
Values sent between devices are 32-bit elements; how exact they have to be, the bound alone decides.
No kernel may reach another device: no remote copies, remote signals or barrier semaphores. Data moves between devices by JAX's collectives and lax.ppermute only.
A program may use at most 192 MiB of HBM per device.

```python
import jax
import jax.numpy as jnp
from jax import lax

D = 1536
HEADS = 48
HEADDIM = 64
STATE = 128
CONV = 4
SPAN = 256
INNER = 3072
LENGTH = 8192
SEQS = 2


def level_of(rng, extent, cuts, low, largest):
    def one(dim, blocks):
        steps = jax.random.uniform(jax.random.fold_in(jax.random.fold_in(rng, 6), dim), (blocks,), jnp.float32, low / len(cuts), largest / len(cuts))
        return jnp.repeat(jnp.exp(steps), extent[dim] // blocks).reshape((-1,) + (1,) * (len(extent) - dim - 1))

    factor_of = one(*cuts[0])
    for cut in cuts[1:]:
        factor_of = factor_of * one(*cut)
    return factor_of


def centred(rng, extent, deviation, most, shards=(), held_as=jnp.bfloat16):
    values = jax.random.normal(rng, extent, jnp.float32) * deviation
    if len(shards) > 0:
        values = level_of(rng, extent, shards, -0.22, 0.18) * values
    return jnp.clip(values, min=-most, max=most).astype(held_as)


def setup_inputs(seed: int = 0) -> dict:
    keys = jax.random.split(jax.random.key(seed), 17)
    hidden = centred(keys[0], (SEQS, LENGTH, D), 1.0, 6.0, ((0, 2), (1, 16)))
    cotangent = centred(keys[1], (SEQS, LENGTH, D), 1.0, 6.0, ((0, 2), (1, 16)))
    norm_gain = jnp.clip(1.0 + 0.18 * jax.random.normal(keys[2], (D,), jnp.float32), 0.1, 1.9)
    w_z = centred(keys[3], (D, INNER), D ** -0.5, 0.15625, ((1, 4),))
    w_x = centred(keys[4], (D, INNER), D ** -0.5, 0.15625, ((1, 4),))
    w_bc = centred(keys[5], (D, 2 * STATE), D ** -0.5, 0.15625)
    w_dt = centred(keys[6], (D, HEADS), (D // 4) ** -0.5, 0.3125, ((1, 4),))
    conv_x = centred(keys[7], (CONV, INNER), CONV ** -0.5, 3.0, ((1, 4),), jnp.float32)
    conv_bc = centred(keys[8], (CONV, 2 * STATE), CONV ** -0.5, 3.0, (), jnp.float32)
    bias_x = centred(keys[9], (INNER,), 0.5, 3.0, ((0, 4),), jnp.float32)
    bias_bc = centred(keys[10], (2 * STATE,), 0.5, 3.0, (), jnp.float32)
    dt_bias = jnp.clip(-6.5 + 2.0 * jax.random.uniform(keys[11], (HEADS,), jnp.float32) ** level_of(keys[11], (HEADS,), ((0, 4),), -0.2, 0.2), -6.5, -4.5)
    a_log = jnp.clip(-4.6 + 5.2999999 * jax.random.uniform(keys[12], (HEADS,), jnp.float32) ** level_of(keys[12], (HEADS,), ((0, 4),), -0.2, 0.2), -4.6, 0.7)
    skip_d = jnp.clip(0.5 + 1.0 * jax.random.uniform(keys[13], (HEADS,), jnp.float32) ** level_of(keys[13], (HEADS,), ((0, 4),), -0.2, 0.2), 0.5, 1.5)
    gain_out = jnp.clip(1.0 + 0.18 * jax.random.normal(keys[14], (INNER,), jnp.float32), 0.1, 1.9)
    w_out = centred(keys[15], (INNER, D), INNER ** -0.5, 0.109375, ((0, 4),))
    return {"hidden": hidden, "cotangent": cotangent, "norm_gain": norm_gain, "w_z": w_z, "w_x": w_x, "w_bc": w_bc, "w_dt": w_dt, "conv_x": conv_x, "conv_bc": conv_bc, "bias_x": bias_x, "bias_bc": bias_bc, "dt_bias": dt_bias, "a_log": a_log, "skip_d": skip_d, "gain_out": gain_out, "w_out": w_out}


epsilon = 1e-05
highest = lax.Precision.HIGHEST

@jax.custom_vjp
def low(v):
    return lax.optimization_barrier(v.astype(jnp.bfloat16)).astype(jnp.float32)

@jax.custom_vjp
def low_back(v):
    return v

def low_keep(v):
    return (low(v), None)

def low_pass(kept, grad):
    return (grad,)

def back_keep(v):
    return (v, None)

def back_low(kept, grad):
    return (low(grad),)
low.defvjp(low_keep, low_pass)
low_back.defvjp(back_keep, back_low)

def causal_conv(edge_rows, rows_now, kernel, bias_row):
    extended = jnp.concatenate([edge_rows, rows_now], axis=0)
    taps_count = kernel.shape[0]
    row_count = rows_now.shape[0]
    summed = jnp.zeros(rows_now.shape, jnp.float32) + bias_row[None, :]
    for offset in range(taps_count):
        summed = summed + kernel[offset][None, :] * extended[offset:offset + row_count]
    return summed

def block_step(carry_state, block_data):
    values, keys_b, reads_c, step_size, log_decay = block_data
    cumulated = jnp.cumsum(log_decay, axis=0)
    positions = jnp.arange(log_decay.shape[0])
    causal = (positions[:, None] >= positions[None, :])[None]
    scores = jnp.dot(reads_c, keys_b.T, precision=highest)
    spread_cum = cumulated.T[:, :, None] - cumulated.T[:, None, :]
    decayed = jnp.where(causal, jnp.exp(jnp.where(causal, spread_cum, 0.0)), 0.0)
    mixing = decayed * scores[None] * step_size.T[:, None, :]
    within = jnp.einsum('hts,shp->thp', mixing, values, precision=highest)
    carried = jnp.einsum('tn,hpn->thp', reads_c, carry_state, precision=highest) * jnp.exp(cumulated)[:, :, None]
    last_cum = cumulated[-1]
    weights = jnp.exp(last_cum[None, :] - cumulated) * step_size
    next_state = jnp.exp(last_cum)[:, None, None] * carry_state + jnp.einsum('sh,shp,sn->hpn', weights, values, keys_b, precision=highest)
    return (next_state, within + carried)

def ssd_outputs(values, keys_b, reads_c, step_size, log_decay, start_state):
    length = values.shape[0]
    blocks = length // SPAN

    def split_rows(member):
        return member.reshape((blocks, SPAN) + member.shape[1:])
    final_state, outputs = lax.scan(jax.checkpoint(block_step), start_state, (split_rows(values), split_rows(keys_b), split_rows(reads_c), split_rows(step_size), split_rows(log_decay)))
    return outputs.reshape(values.shape)

def layer_forward(rows_in, packed):
    norm_gain, w_z, w_x, w_bc, w_dt, conv_x, conv_bc, bias_x, bias_bc, dt_bias, a_log, skip_d, gain_out, w_out = packed
    length = rows_in.shape[0]
    scale_in = lax.rsqrt(lax.optimization_barrier(jnp.mean(rows_in * rows_in, axis=1, keepdims=True)) + epsilon)
    normed = low(rows_in * scale_in * norm_gain)
    gate_z = low_back(jnp.dot(normed, w_z, precision=highest))
    inner_x = low_back(jnp.dot(normed, w_x, precision=highest))
    inner_bc = low_back(jnp.dot(normed, w_bc, precision=highest))
    step_raw = low_back(jnp.dot(normed, w_dt, precision=highest))
    pre_x = causal_conv(jnp.zeros((CONV - 1, inner_x.shape[1]), jnp.float32), inner_x, conv_x, bias_x)
    pre_bc = causal_conv(jnp.zeros((CONV - 1, inner_bc.shape[1]), jnp.float32), inner_bc, conv_bc, bias_bc)
    act_x = jax.nn.silu(pre_x)
    act_bc = jax.nn.silu(pre_bc)
    values = low(act_x).reshape(length, HEADS, HEADDIM)
    bc_low = low(act_bc)
    keys_b = bc_low[:, :STATE]
    reads_c = bc_low[:, STATE:]
    step_size = jax.nn.softplus(step_raw + dt_bias[None, :])
    log_decay = -jnp.exp(a_log)[None, :] * step_size
    start_state = jnp.zeros((HEADS, HEADDIM, STATE), jnp.float32)
    ssd_rows = ssd_outputs(values, keys_b, reads_c, step_size, log_decay, start_state)
    mixed_out = low_back(ssd_rows.reshape(length, HEADS * HEADDIM) + jnp.repeat(skip_d, HEADDIM)[None, :] * act_x)
    gated_out = mixed_out * jax.nn.silu(gate_z)
    scale_out = lax.rsqrt(lax.optimization_barrier(jnp.mean(gated_out * gated_out, axis=1, keepdims=True)) + epsilon)
    normed_out = low(gated_out * scale_out * gain_out)
    return rows_in + jnp.dot(normed_out, w_out, precision=highest)

def reference(hidden, cotangent, norm_gain, w_z, w_x, w_bc, w_dt, conv_x, conv_bc, bias_x, bias_bc, dt_bias, a_log, skip_d, gain_out, w_out):
    packed = (norm_gain.astype(jnp.float32), w_z.astype(jnp.float32), w_x.astype(jnp.float32), w_bc.astype(jnp.float32), w_dt.astype(jnp.float32), conv_x.astype(jnp.float32), conv_bc.astype(jnp.float32), bias_x.astype(jnp.float32), bias_bc.astype(jnp.float32), dt_bias.astype(jnp.float32), a_log.astype(jnp.float32), skip_d.astype(jnp.float32), gain_out.astype(jnp.float32), w_out.astype(jnp.float32))

    def one_sequence(totals, pair_data):
        seq_rows, seq_cot = pair_data
        result_rows, pull_back = jax.vjp(layer_forward, seq_rows.astype(jnp.float32), packed)
        grad_rows, grad_packed = pull_back(seq_cot.astype(jnp.float32))
        new_totals = jax.tree.map(jnp.add, totals, grad_packed)
        return (new_totals, (result_rows.astype(jnp.bfloat16), grad_rows.astype(jnp.bfloat16)))
    start_totals = jax.tree.map(jnp.zeros_like, packed)
    totals, results = lax.scan(one_sequence, start_totals, (hidden, cotangent))
    return (results[0], results[1], totals[0], totals[1], totals[2], totals[3], totals[4], totals[5], totals[6], totals[7], totals[8], totals[9], totals[10], totals[11], totals[12], totals[13])
```

```python
import functools

import jax
import jax.numpy as jnp
from jax import lax
from jax.experimental import pallas as pl
from jax.experimental.pallas import tpu as pltpu
from jax.sharding import PartitionSpec as P

HEADDIM = 64
STATE = 128
CHUNK = 128
LANES = 128
EDGE = 8

epsilon = 1e-05
f32 = jnp.float32
bf16 = jnp.bfloat16


def low(value):
    return value.astype(bf16)


def dot(left, right):
    return jnp.dot(left, right, preferred_element_type=f32)


def dot_nt(left, right):
    return lax.dot_general(left, right, (((1,), (1,)), ((), ())), preferred_element_type=f32)


def dot_tn(left, right):
    return lax.dot_general(left, right, (((0,), (0,)), ((), ())), preferred_element_type=f32)


def parts_of(value, count):
    terms = []
    for _ in range(count):
        term = value.astype(bf16)
        terms.append(term)
        value = value - term.astype(f32)
    return terms


def head_map(width):
    head = lax.broadcasted_iota(jnp.int32, (LANES, width), 0)
    column = lax.broadcasted_iota(jnp.int32, (LANES, width), 1)
    return (lax.shift_right_logical(column, 6) == head).astype(f32).astype(bf16)


def spread(per_head, heads):
    high, rest = parts_of(per_head, 2)
    return dot(high, heads) + dot(rest, heads)


def per_head_sum(channels, heads):
    high, rest = parts_of(channels, 2)
    return dot_nt(high, heads) + dot_nt(rest, heads)


def running(mask, value):
    terms = parts_of(value, 3)
    return dot(mask, terms[0]) + dot(mask, terms[1]) + dot(mask, terms[2])


def as_row(vector):
    return vector[...].reshape(1, vector.shape[0])


def row_col():
    row = lax.broadcasted_iota(jnp.int32, (CHUNK, CHUNK), 0)
    column = lax.broadcasted_iota(jnp.int32, (CHUNK, CHUNK), 1)
    return row, column


def as_mask(where):
    return where.astype(f32).astype(bf16)


def sigmoid(value):
    return 1.0 / (1.0 + jnp.exp(-value))


def silu(value):
    return value * sigmoid(value)


def silu_slope(value):
    sigma = sigmoid(value)
    return sigma * (1.0 + value * (1.0 - sigma))


def softplus(value):
    return jnp.maximum(value, 0.0) + jnp.log1p(jnp.exp(-jnp.abs(value)))


def column_sum(value):
    return jnp.sum(value, axis=0, keepdims=True)


def row_sum(value):
    return jnp.sum(value, axis=1, keepdims=True)


def exp_below(where, value):
    return jnp.exp(jnp.where(where, value, -1e30))


def project_kernel(hid, gain, wx, wbc, wdt, normed, normed32, inx, inbc, sraw, edge):
    rows = hid[...].astype(f32)
    scale = lax.rsqrt(jnp.mean(rows * rows, axis=1, keepdims=True) + epsilon)
    value = low(rows * scale * as_row(gain))
    normed[...] = value
    normed32[...] = value.astype(f32)
    width = inx.shape[1]
    inx[...] = dot(value, wx[...])
    inbc[...] = dot(value, wbc[...])
    edge[:, :width] = inx[CHUNK - EDGE :, :]
    edge[:, width:] = inbc[CHUNK - EDGE :, :]
    sraw[...] = jnp.zeros(sraw.shape, f32)
    sraw[:, : wdt.shape[0]] = dot_nt(value, wdt[...])


def conv_rows(ext, taps, bias):
    total = as_row(bias) + taps[0:1, :] * ext[pl.ds(EDGE - 3, CHUNK), :]
    for k in range(1, 4):
        total = total + taps[k : k + 1, :] * ext[pl.ds(EDGE - 3 + k, CHUNK), :]
    return total


def front_kernel(
    edge, inx, inbc, sraw, cx, cbc, bx, bbc, small,
    prex, prebc, step_out, cumc_out, cumd_out, starts, payload,
    extx, extbc, state, base,
):
    i = pl.program_id(0)
    width = inx.shape[1]

    @pl.when(i == 0)
    def _():
        extx[0:EDGE, :] = edge[:, :width]
        extbc[0:EDGE, :] = edge[:, width:]
        state[...] = jnp.zeros(state.shape, f32)
        base[...] = jnp.zeros(base.shape, f32)

    @pl.when(i > 0)
    def _():
        extx[0:EDGE, :] = extx[CHUNK : CHUNK + EDGE, :]
        extbc[0:EDGE, :] = extbc[CHUNK : CHUNK + EDGE, :]

    extx[EDGE:, :] = inx[...]
    extbc[EDGE:, :] = inbc[...]
    pre_x = conv_rows(extx, cx, bx)
    pre_bc = conv_rows(extbc, cbc, bbc)
    prex[...] = pre_x
    prebc[...] = pre_bc
    values = low(silu(pre_x)).astype(f32)
    keys_t = jnp.transpose(low(silu(pre_bc[:, :STATE])).astype(f32))
    step = softplus(sraw[...] + small[0:1, :])
    decay = -jnp.exp(small[1:2, :]) * step
    row, column = row_col()
    cumc = running(as_mask(row >= column), decay)
    last = cumc[CHUNK - 1 : CHUNK, :]
    step_out[...] = step
    cumc_out[...] = cumc
    cumd_out[...] = cumc + base[0:1, :]
    starts[0] = state[...]
    heads = head_map(width)
    weights = spread(jnp.exp(last - cumc) * step, heads)
    keep = spread(jnp.exp(jnp.broadcast_to(last, (EDGE, LANES))), heads)[0:1, :]
    state[...] = keep * state[...] + dot(low(keys_t), low(values * weights))
    base[...] = base[...] + last

    @pl.when(i == pl.num_programs(0) - 1)
    def _():
        payload[:, :width] = state[...]
        payload[:, width:] = jnp.broadcast_to(base[0:1, :], (STATE, LANES))


def scan_kernel(parts, ranges, received, incoming, decays):
    width = incoming.shape[1]
    decays[...] = spread(jnp.exp(received[:, width:]), head_map(width))
    carry = jnp.zeros((parts, width), f32)
    for i in range(ranges):
        here = slice(i * parts, (i + 1) * parts)
        incoming[here, :] = carry
        carry = decays[here, :] * carry + received[here, :width]


def scan_back_kernel(parts, ranges, received, decays, incoming):
    carry = jnp.zeros((parts, incoming.shape[1]), f32)
    for i in reversed(range(ranges)):
        here = slice(i * parts, (i + 1) * parts)
        incoming[here, :] = carry
        carry = decays[here, :] * carry + received[here, :]


def within_kernel(prex, prebc, step_in, cumc_in, starts, out):
    width = prex.shape[1]
    heads = head_map(width)
    values = low(silu(prex[...])).astype(f32)
    act_bc = low(silu(prebc[...]))
    keys, reads = act_bc[:, :STATE], act_bc[:, STATE:]
    step, cumc = step_in[...], cumc_in[...]
    cum_t = jnp.transpose(cumc)
    scaled = values * spread(step, heads)
    carried = spread(jnp.exp(cumc), heads) * dot(reads, low(starts[0]))
    scores = dot_nt(reads, keys)
    row, column = row_col()
    causal = row >= column
    first = lax.broadcasted_iota(jnp.int32, (CHUNK, LANES), 1) < HEADDIM
    for pair in range(width // LANES):
        lanes = slice(pair * LANES, (pair + 1) * LANES)
        pieces = []
        for h in (2 * pair, 2 * pair + 1):
            decayed = exp_below(causal, cumc[:, h : h + 1] - cum_t[h : h + 1, :])
            pieces.append(low(decayed * scores))
        here = scaled[:, lanes]
        stacked = jnp.concatenate(
            [low(jnp.where(first, here, 0.0)), low(jnp.where(first, 0.0, here))], axis=0
        )
        out[:, lanes] = carried[:, lanes] + dot(jnp.concatenate(pieces, axis=1), stacked)


def mix_kernel(incoming, prex, prebc, cumd, within, gate_z, d_out, small, gain, mixed_out, sums):
    width = prex.shape[1]
    heads = head_map(width)
    reads = low(silu(prebc[:, STATE:]))
    ssd = within[...] + spread(jnp.exp(cumd[...]), heads) * dot(reads, low(incoming[...]))
    skip = spread(small[...], heads)[2:3, :]
    mixed = ssd + skip * silu(prex[...])
    mixed_out[...] = mixed
    gated = mixed * silu(gate_z[...])
    squares = row_sum(gated * gated)
    products = row_sum(d_out[...] * as_row(gain) * gated)
    column = lax.broadcasted_iota(jnp.int32, (CHUNK, LANES), 1)
    both = jnp.where(column == 0, squares, jnp.where(column == 1, products, 0.0))
    sums[...] = jnp.broadcast_to(jnp.transpose(both)[0:2, :][None], sums.shape)


def gate_kernel(
    inner_all, totals, mixed_in, gate_z, d_out, prex, prebc, cumd, small, gain,
    normed_out, gate_low, d_mixed, col_out, payload,
):
    i = pl.program_id(0)
    width = prex.shape[1]
    heads = head_map(width)

    @pl.when(i == 0)
    def _():
        col_out[...] = jnp.zeros(col_out.shape, f32)
        payload[...] = jnp.zeros(payload.shape, f32)

    all_sums = totals[0]
    for k in range(1, totals.shape[0]):
        all_sums = all_sums + totals[k]
    squares, products = (
        jnp.transpose(jnp.broadcast_to(all_sums[r : r + 1, :], (CHUNK, CHUNK)))[:, 0:1]
        for r in range(2)
    )
    scale = lax.rsqrt(squares / inner_all + epsilon)
    mean_dot = scale * products / inner_all
    gate = gate_z[...]
    sigma = sigmoid(gate)
    silu_z = gate * sigma
    mixed = mixed_in[...]
    unit = mixed * silu_z * scale
    d_normed = d_out[...]
    gain_row = as_row(gain)
    out_low = low(unit * gain_row)
    normed_out[...] = out_low
    d_gated = scale * (d_normed * gain_row - unit * mean_dot)
    g_low = low(d_gated * silu_z)
    d_mixed[...] = g_low
    slope = sigma * (1.0 + gate * (1.0 - sigma))
    gate_grad = low(d_gated * mixed * slope)
    gate_low[...] = gate_grad
    g = g_low.astype(f32)
    col_out[0:1, :] += column_sum(d_normed * unit)
    col_out[1:2, :] += column_sum(g * silu(prex[...]))
    reads_t = jnp.transpose(low(silu(prebc[:, STATE:])).astype(f32))
    payload[...] += dot(low(reads_t), low(g * spread(jnp.exp(cumd[...]), heads)))


def back_kernel(
    prex, prebc, step_in, cumc_in, cumd, starts, incoming, d_mixed,
    d_values, d_bc, d_step, d_log, full_starts,
    later, gy_t,
):
    i = pl.program_id(0)
    width = prex.shape[1]
    heads = head_map(width)

    @pl.when(i == 0)
    def _():
        later[...] = jnp.zeros(later.shape, f32)
        gy_t[...] = jnp.zeros(gy_t.shape, f32)

    values_low = low(silu(prex[...]))
    values = values_low.astype(f32)
    act_bc = low(silu(prebc[...]))
    keys, reads = act_bc[:, :STATE], act_bc[:, STATE:]
    step, cumc = step_in[...], cumc_in[...]
    cum_t = jnp.transpose(cumc)
    last = cumc[CHUNK - 1 : CHUNK, :]
    before = cumd[CHUNK - 1 : CHUNK, :] - last
    tops = jnp.concatenate(
        [jnp.broadcast_to(before, (EDGE, LANES)), jnp.broadcast_to(last, (EDGE, LANES))], axis=0
    )
    tops = spread(jnp.exp(tops), heads)
    start = starts[0] + tops[0:1, :] * incoming[...]
    full_starts[0] = start
    keep = tops[EDGE : EDGE + 1, :]
    start_low = low(start)
    step_wide = spread(step, heads)
    out_wide = spread(jnp.exp(last - cumc), heads)
    g_low = d_mixed[...]
    g = g_low.astype(f32)
    g_in = g * spread(jnp.exp(cumc), heads)
    g_in_low = low(g_in)

    row, column = row_col()
    causal = row <= column
    scores_t = dot_nt(keys, reads)
    first = lax.broadcasted_iota(jnp.int32, (CHUNK, LANES), 1) < HEADDIM
    d_scores_t = jnp.zeros((CHUNK, CHUNK), f32)
    step_within = jnp.zeros((CHUNK, LANES), f32)
    later_low = low(later[...])
    onward = out_wide * dot(keys, later_low)
    for pair in range(width // LANES):
        lanes = slice(pair * LANES, (pair + 1) * LANES)
        g_pair = g[:, lanes]
        halves = (low(jnp.where(first, g_pair, 0.0)), low(jnp.where(first, 0.0, g_pair)))
        pieces = []
        for h, g_half in zip((2 * pair, 2 * pair + 1), halves):
            decayed = exp_below(causal, cum_t[h : h + 1, :] - cumc[:, h : h + 1])
            d_mixing = dot_nt(values_low[:, lanes], g_half)
            weighted = decayed * d_mixing
            step_col = step[:, h : h + 1]
            d_scores_t = d_scores_t + weighted * step_col
            product = weighted * scores_t
            step_within = step_within + jnp.where(column == h, row_sum(product), 0.0)
            gy_t[h : h + 1, :] = column_sum(product * step_col)
            pieces.append(low(decayed * scores_t))
        d_pair = dot(jnp.concatenate(pieces, axis=1), jnp.concatenate(halves, axis=0))
        d_values[:, lanes] = step_wide[:, lanes] * (d_pair + onward[:, lanes])

    d_keys = dot(low(d_scores_t), reads) + dot_nt(low(values * step_wide * out_wide), later_low)
    d_reads = dot(low(jnp.transpose(d_scores_t)), keys) + dot_nt(g_in_low, start_low)
    d_bc[:, :STATE] = d_keys
    d_bc[:, STATE:] = d_reads
    from_start = per_head_sum(g_in * dot(reads, start_low), heads)
    step_onward = per_head_sum(values * onward, heads)
    d_step[...] = step_within + step_onward
    across = column_sum(start * later[...])
    across = per_head_sum(jnp.broadcast_to(across, (EDGE, width)), heads)[0:1, :] * jnp.exp(last)
    inside = jnp.transpose(gy_t[...]) - step * step_within + from_start
    d_log[...] = (
        running(as_mask(row <= column), inside)
        + running(as_mask(row > column), step * step_onward)
        + across
    )
    later[...] = keep * later[...] + dot(low(jnp.transpose(reads.astype(f32))), g_in_low)


def edge_kernel(incoming, prex, prebc, step_in, cumd, total, d_mixed, d_values, d_bc, small, out):
    width = prex.shape[1]
    heads = head_map(width)
    low_in = low(incoming[...])
    act_bc = low(silu(prebc[...]))
    step = step_in[...]
    weight = spread(step * jnp.exp(total[EDGE - 1 : EDGE, :] - cumd[...]), heads)
    skip = spread(small[...], heads)[2:3, :]
    values = low(silu(prex[...])).astype(f32)
    d_val = d_values[...] + weight * dot(act_bc[:, :STATE], low_in)
    d_keys = d_bc[:, :STATE] + dot_nt(low(values * weight), low_in)
    d_act = d_val + skip * d_mixed[...].astype(f32)[:EDGE]
    out[:, :width] = d_act * silu_slope(prex[...])
    out[:, width : width + STATE] = d_keys * silu_slope(prebc[:, :STATE])
    out[:, width + STATE :] = d_bc[:, STATE:] * silu_slope(prebc[:, STATE:])


def conv_back(chunk, ext, inner, before, edge, taps, d_pre, sums, columns):
    ext[0:CHUNK, :] = d_pre
    d_inner = taps[3:4, :] * d_pre
    for k in range(3):
        d_inner = d_inner + taps[k : k + 1, :] * ext[pl.ds(3 - k, CHUNK), :]
    ext[CHUNK:, :] = ext[0:EDGE, :]
    rows = jnp.where(chunk == 0, edge, before[...])
    inner[0:EDGE, :] = rows
    for k in range(4):
        sums[k : k + 1, columns] += column_sum(d_pre * inner[pl.ds(EDGE - 3 + k, CHUNK), :])
    sums[4:5, columns] += column_sum(d_pre)
    return d_inner


def finish_kernel(
    core, incoming, full_starts, prex, prebc, inx, inbc, before_x, before_bc, edge, edge_next,
    sraw, step_in, cumc_in, cumd_in, total, d_mixed, d_values, d_bc, d_step, d_log, cx, cbc, small,
    col_in,
    x_low, own, send, bc_low, bc_rows, step_out, sums,
    ext_x, ext_bc, inner_x, inner_bc,
):
    i = pl.program_id(0)
    chunk = pl.num_programs(0) - 1 - i
    width = prex.shape[1]
    half = width // 2
    heads = head_map(width)

    @pl.when(i == 0)
    def _():
        ext_x[CHUNK:, :] = edge_next[:, :width]
        ext_bc[CHUNK:, :] = edge_next[:, width:]
        sums[...] = jnp.zeros(sums.shape, f32)
        sums[5:7, :width] = col_in[0:2, :]

    late = incoming[...]
    late_low = low(late)
    act_bc = low(silu(prebc[...]))
    keys = act_bc[:, :STATE]
    pre_x = prex[...]
    sigma = sigmoid(pre_x)
    slope_x = sigma * (1.0 + pre_x * (1.0 - sigma))
    values = low(pre_x * sigma).astype(f32)
    step, cumd = step_in[...], cumd_in[...]
    end = total[EDGE - 1 : EDGE, :]
    step_wide = spread(step, heads)
    out_wide = spread(jnp.exp(end - cumd), heads)
    skip = spread(small[...], heads)[2:3, :]
    onward = out_wide * dot(keys, late_low)
    d_val = d_values[...] + step_wide * onward
    d_keys = d_bc[:, :STATE] + dot_nt(low(values * step_wide * out_wide), late_low)
    step_onward = per_head_sum(values * onward, heads)
    before = cumd[CHUNK - 1 : CHUNK, :] - cumc_in[CHUNK - 1 : CHUNK, :]
    across = column_sum(full_starts[0] * late)
    across = per_head_sum(jnp.broadcast_to(across, (EDGE, width)), heads)[0:1, :]
    row, column = row_col()
    log_grad = (
        d_log[...]
        + running(as_mask(row > column), step * step_onward)
        + across * jnp.exp(end - before)
    )
    rate = jnp.exp(small[1:2, :])
    step_grad = d_step[...] + step_onward - rate * log_grad
    raw = sraw[...] + small[0:1, :]
    step_pre = step_grad * sigmoid(raw)
    for_heads = slice(width + 2 * STATE, width + 2 * STATE + LANES)
    sums[0:1, for_heads] += column_sum(log_grad * (-rate * step))
    sums[1:2, for_heads] += column_sum(step_pre)
    step_out[...] = low(step_pre)

    d_pre_x = (d_val + skip * d_mixed[...].astype(f32)) * slope_x
    inner_x[EDGE:, :] = inx[...]
    of_x = slice(0, width)
    d_in = low(
        conv_back(chunk, ext_x, inner_x, before_x, edge[:, of_x], cx, d_pre_x, sums, of_x)
    )
    x_low[...] = d_in
    wide = d_in.astype(f32)
    is_first = core[0] == 0
    own[...] = low(jnp.where(is_first, wide[:, :half], wide[:, half:]))
    send[...] = jnp.where(is_first, wide[:, half:], wide[:, :half])

    d_act_bc = jnp.concatenate([d_keys, d_bc[:, STATE:]], axis=1)
    d_pre_bc = d_act_bc * silu_slope(prebc[...])
    inner_bc[EDGE:, :] = inbc[...]
    of_bc = slice(width, width + 2 * STATE)
    d_in = conv_back(
        chunk, ext_bc, inner_bc, before_bc, edge[:, of_bc], cbc, d_pre_bc, sums, of_bc
    )
    bc_low[...] = low(d_in)
    shares = jnp.transpose(d_in)
    share = bc_rows.shape[1]
    for k in range(bc_rows.shape[0]):
        bc_rows[k] = shares[k * share : (k + 1) * share, :]


def norm_back_kernel(
    dg, dx, dbc, dst, ahead, hid, hid_block, gain, wz, wx, wbc, wdt, wout, sums, bc_rows, out, parts, scale, along, gains
):
    i = pl.program_id(0)
    last = pl.num_programs(0) - 1
    _, count, width = out.shape

    @pl.when(i == 0)
    def _():
        rows = hid[...].astype(f32)
        mean = jnp.mean(rows * rows, axis=1, keepdims=True)
        scale[...] = jnp.broadcast_to(lax.rsqrt(mean + epsilon), scale.shape)
        along[...] = jnp.zeros(along.shape, f32)

    total = dot_nt(dg[...], wz[...]) + dot_nt(dx[...], wx[...])
    total = total + dot_nt(dbc[...], wbc[...])
    total = total + dot(dst[:, : wdt.shape[0]], wdt[...])
    out[0] = dot(ahead[...], wout[...])
    out[1] = total
    product = total * (hid_block[...].astype(f32) * scale[:, 0:1])
    here = pl.ds(pl.multiple_of(i * width, width), width)
    gains[0:1, here] = column_sum(product)
    weighted = product * as_row(gain)
    partial = weighted[:, :LANES]
    for k in range(1, width // LANES):
        partial = partial + weighted[:, k * LANES : (k + 1) * LANES]
    along[...] += partial

    @pl.when(i == last)
    def _():
        heads, share = bc_rows.shape[0], bc_rows.shape[1]
        first = dg.shape[1]
        own = gains.shape[1] // heads
        parts[...] = jnp.zeros(parts.shape, f32)
        for k in range(heads):
            parts[k, :share, :] = bc_rows[k]
            parts[k, share : share + 5, : 2 * STATE] = sums[0:5, first : first + 2 * STATE]
            parts[k, share + 5 : share + 6, :own] = gains[0:1, k * own : (k + 1) * own]
        for j in range(count // CHUNK):
            lanes = slice(j * CHUNK, (j + 1) * CHUNK)
            line = column_sum(jnp.transpose(along[lanes, :]))
            for k in range(heads):
                parts[k, share + 6 : share + 7, lanes] = line


def share_kernel(buffer, parts, step_low, normed, sums, out, dots):
    share = parts[0]
    for k in range(1, parts.shape[0]):
        share = share + parts[k]
    count = share.shape[0] - EDGE
    extra = share[count:, :]
    dots[...] = extra
    features = normed.shape[1]
    own = features // parts.shape[0]
    width = features // 2
    gains = jnp.concatenate([extra[5:6, :own], jnp.zeros((1, features - own), f32)], axis=1)
    lane = lax.broadcasted_iota(jnp.int32, (EDGE, features), 1)
    row = lax.broadcasted_iota(jnp.int32, (EDGE, features), 0)
    of_bc = (lane >= width) & (lane < width + 2 * STATE) & (row < 5)
    summed = jnp.concatenate(
        [
            jnp.zeros((EDGE, width), f32),
            extra[:, : 2 * STATE],
            jnp.zeros((EDGE, features - width - 2 * STATE), f32),
        ],
        axis=1,
    )
    tiny = jnp.where(row == 7, gains, jnp.where(of_bc, summed, sums[...]))
    steps = 2 * EDGE
    of_w = dot(low(share[:count, :]), normed[...])
    of_dt = dot_tn(step_low[...], normed[...])[:steps, :]
    ranges, rows, half = out.shape
    spare = jnp.zeros((rows * ranges * half // features - count - steps - EDGE, features), f32)
    stacked = jnp.concatenate([of_w, of_dt, tiny, spare], axis=0)
    blocks = features // half
    per = ranges // blocks
    for k in range(blocks):
        out[k * per : (k + 1) * per] = stacked[:, k * half : (k + 1) * half].reshape(per, rows, half)


def copy_kernel(source, out):
    out[...] = source[...]


def join_kernel(core, mine, theirs, out):
    half = mine.shape[2]
    per = mine.shape[0]
    count = out.shape[0] // per
    own = mine[:, :count, :].reshape(per * count, half)
    other = theirs[:, :count, :].reshape(per * count, half)
    out[:, :half] = jnp.where(core[0] == 0, own, other)
    out[:, half:] = jnp.where(core[0] == 0, other, own)


def deal_kernel(
    mine, theirs, bc, dt, conv_x, conv_bc, bias_x, bias_bc, gain, norm_gain, by_head, sums
):
    share, steps = bc.shape[0], dt.shape[0]
    taps, width = conv_x.shape
    bc_width = conv_bc.shape[1]
    total = mine[...] + theirs[...]
    ranges, count, half = total.shape
    blocks = bc.shape[1] // half
    per = ranges // blocks
    first = share + 2 * EDGE
    for k in range(blocks):
        lanes = slice(k * half, (k + 1) * half)
        block = total[k * per : (k + 1) * per].reshape(per * count, half)
        bc[:, lanes] = block[:share, :]
        dt[:, lanes] = block[share : share + steps, :]
        sums[:, lanes] = block[first : first + EDGE, :]
    conv_x[...] = sums[:taps, :width]
    bias_x[...] = sums[taps, :width]
    conv_bc[...] = sums[:taps, width : width + bc_width]
    bias_bc[...] = sums[taps, width : width + bc_width]
    gain[...] = sums[5, :width]
    norm_gain[...] = sums[7, : norm_gain.shape[0]]
    by_head[...] = sums[:, width + bc_width : width + bc_width + LANES]
    by_head[2:3, :] = per_head_sum(sums[:, :width], head_map(width))[6:7, :]


def product_kernel(left, right, out):
    out[...] = dot_tn(left[...], right[...])


def outer_kernel(left, right, left_peer, right_peer, out):
    product = dot_tn(left[...], right[...]) + dot_tn(low(left_peer[...]), low(right_peer[...]))
    per, _, half = out.shape
    count = product.shape[0] // per
    out[:, :count, :] = product.reshape(per, count, half)


def total_kernel(parts, out):
    total = parts[0]
    for k in range(1, parts.shape[0]):
        total = total + parts[k]
    out[...] = jnp.broadcast_to(total[None], out.shape)


def whole(shape):
    return pl.BlockSpec(shape, lambda i: (0,) * len(shape))


def call(kernel, grid, ins, outs, scratch=(), flops=0, moved=0, megabytes=58, aliases=None):
    return pl.pallas_call(
        kernel,
        grid=(grid,),
        in_specs=[spec for _, spec in ins],
        out_specs=[spec for _, _, spec in outs],
        out_shape=[jax.ShapeDtypeStruct(shape, kind) for shape, kind, _ in outs],
        scratch_shapes=list(scratch),
        input_output_aliases=aliases or {},
        compiler_params=pltpu.CompilerParams(
            dimension_semantics=("arbitrary",), vmem_limit_bytes=megabytes * 2**20
        ),
        cost_estimate=pl.CostEstimate(flops=flops, bytes_accessed=moved, transcendentals=0),
    )(*[array for array, _ in ins])


def from_behind(shard, axis, by):
    peers = lax.axis_size(axis)
    pairs = [(i, i + by) for i in range(peers) if 0 <= i + by < peers]
    return lax.ppermute(shard, axis, pairs)


def swap_cores(shard):
    return lax.ppermute(shard, "dp", [(0, 1), (1, 0)])


def per_device(
    hidden,
    cotangent,
    norm_gain,
    w_z,
    w_x,
    w_bc,
    w_dt,
    conv_x,
    conv_bc,
    bias_x,
    bias_bc,
    dt_bias,
    a_log,
    skip_d,
    gain_out,
    w_out,
):
    hid, cot = hidden[0], cotangent[0]
    tokens, model_width = hid.shape
    heads_here = w_dt.shape[1]
    width = w_z.shape[1]
    half = width // 2
    bc_width = w_bc.shape[1]
    parts_head = lax.axis_size("head")
    bc_share = bc_width // parts_head
    chunks = tokens // CHUNK
    ranges = lax.axis_size("seq")
    parts = STATE // ranges
    head_pos = lax.axis_index("head")
    core = lax.axis_index("dp").astype(jnp.int32)
    core_flag = core.reshape(1)
    flag_spec = pl.BlockSpec(memory_space=pltpu.SMEM)

    def rows_of(count, columns):
        return pl.BlockSpec((count, columns), lambda i: (i, 0))

    def rows(columns):
        return rows_of(CHUNK, columns)

    def rows_back(columns):
        return pl.BlockSpec((CHUNK, columns), lambda i: (chunks - 1 - i, 0))

    pair_line = pl.BlockSpec((parts_head, 2, CHUNK), lambda i: (0, 0, i))
    state_spec = pl.BlockSpec((1, STATE, width), lambda i: (i, 0, 0))
    state_back = pl.BlockSpec((1, STATE, width), lambda i: (chunks - 1 - i, 0, 0))
    dt_rows = w_dt.T
    small = jnp.pad(
        jnp.stack([dt_bias, a_log, skip_d]), ((0, EDGE - 3), (0, LANES - heads_here))
    )
    small_spec = whole((EDGE, LANES))

    normed, normed32, inner_x, inner_bc, step_raw, edge = call(
        project_kernel,
        chunks,
        [
            (hid, rows(model_width)),
            (norm_gain, whole((model_width,))),
            (w_x, whole(w_x.shape)),
            (w_bc, whole(w_bc.shape)),
            (dt_rows, whole(dt_rows.shape)),
        ],
        [
            ((tokens, model_width), bf16, rows(model_width)),
            ((tokens, model_width), f32, rows(model_width)),
            ((tokens, width), f32, rows(width)),
            ((tokens, bc_width), f32, rows(bc_width)),
            ((tokens, LANES), f32, rows(LANES)),
            ((EDGE, width + bc_width), f32, whole((EDGE, width + bc_width))),
        ],
        flops=2 * tokens * model_width * (width + bc_width),
        moved=18 << 20,
    )
    edge = from_behind(edge, "seq", 1)
    gate_z = jnp.dot(normed, w_z, preferred_element_type=f32)
    d_out = jnp.einsum("td,id->ti", cot, w_out, preferred_element_type=f32)
    normed_peer = swap_cores(normed32)

    pre_x, pre_bc, step, cumc, cumd, starts, payload = call(
        front_kernel,
        chunks,
        [
            (edge, whole((EDGE, width + bc_width))),
            (inner_x, rows(width)),
            (inner_bc, rows(bc_width)),
            (step_raw, rows(LANES)),
            (conv_x, whole(conv_x.shape)),
            (conv_bc, whole(conv_bc.shape)),
            (bias_x, whole((width,))),
            (bias_bc, whole((bc_width,))),
            (small, small_spec),
        ],
        [
            ((tokens, width), f32, rows(width)),
            ((tokens, bc_width), f32, rows(bc_width)),
            ((tokens, LANES), f32, rows(LANES)),
            ((tokens, LANES), f32, rows(LANES)),
            ((tokens, LANES), f32, rows(LANES)),
            ((chunks, STATE, width), f32, state_spec),
            ((STATE, width + LANES), f32, whole((STATE, width + LANES))),
        ],
        [
            pltpu.VMEM((CHUNK + EDGE, width), f32),
            pltpu.VMEM((CHUNK + EDGE, bc_width), f32),
            pltpu.VMEM((STATE, width), f32),
            pltpu.VMEM((EDGE, LANES), f32),
        ],
        flops=2 * tokens * STATE * width,
        moved=8 << 20,
    )

    def exchanged(array):
        blocks = array.reshape(ranges, parts, array.shape[1])
        return lax.all_to_all(blocks, "seq", 0, 0).reshape(array.shape)

    received = exchanged(payload)
    within = call(
        within_kernel,
        chunks,
        [
            (pre_x, rows(width)),
            (pre_bc, rows(bc_width)),
            (step, rows(LANES)),
            (cumc, rows(LANES)),
            (starts, state_spec),
        ],
        [((tokens, width), f32, rows(width))],
        flops=6 * tokens * CHUNK * width,
        moved=8 << 20,
    )[0]
    incoming, decays = call(
        functools.partial(scan_kernel, parts, ranges),
        1,
        [(received, whole(received.shape))],
        [((STATE, width), f32, whole((STATE, width)))] * 2,
        moved=1 << 20,
    )
    incoming = exchanged(incoming)

    mixed, sums = call(
        mix_kernel,
        chunks,
        [
            (incoming, whole((STATE, width))),
            (pre_x, rows(width)),
            (pre_bc, rows(bc_width)),
            (cumd, rows(LANES)),
            (within, rows(width)),
            (gate_z, rows(width)),
            (d_out, rows(width)),
            (small, small_spec),
            (gain_out, whole((width,))),
        ],
        [((tokens, width), f32, rows(width)), ((parts_head, 2, tokens), f32, pair_line)],
        flops=2 * tokens * STATE * width,
        moved=10 << 20,
    )
    totals = lax.all_to_all(sums, "head", 0, 0)
    normed_out, gate_low, d_mixed, col_out, payload = call(
        functools.partial(gate_kernel, width * parts_head),
        chunks,
        [
            (totals, pair_line),
            (mixed, rows(width)),
            (gate_z, rows(width)),
            (d_out, rows(width)),
            (pre_x, rows(width)),
            (pre_bc, rows(bc_width)),
            (cumd, rows(LANES)),
            (small, small_spec),
            (gain_out, whole((width,))),
        ],
        [
            ((tokens, width), bf16, rows(width)),
            ((tokens, width), bf16, rows(width)),
            ((tokens, width), bf16, rows(width)),
            ((EDGE, width), f32, whole((EDGE, width))),
            ((STATE, width), f32, whole((STATE, width))),
        ],
        flops=2 * tokens * STATE * width,
        moved=14 << 20,
    )

    received = exchanged(payload)
    share = model_width // parts_head
    d_values, d_bc, d_step, d_log, full_starts = call(
        back_kernel,
        chunks,
        [
            (pre_x, rows_back(width)),
            (pre_bc, rows_back(bc_width)),
            (step, rows_back(LANES)),
            (cumc, rows_back(LANES)),
            (cumd, rows_back(LANES)),
            (starts, state_back),
            (incoming, whole((STATE, width))),
            (d_mixed, rows_back(width)),
        ],
        [
            ((tokens, width), f32, rows_back(width)),
            ((tokens, bc_width), f32, rows_back(bc_width)),
            ((tokens, LANES), f32, rows_back(LANES)),
            ((tokens, LANES), f32, rows_back(LANES)),
            ((chunks, STATE, width), f32, state_back),
        ],
        [pltpu.VMEM((STATE, width), f32), pltpu.VMEM((LANES, CHUNK), f32)],
    )
    half_columns = pl.BlockSpec((tokens, half), lambda i: (0, i))
    pair_columns = pl.BlockSpec((tokens, 2 * LANES), lambda i: (0, i))
    grad_z = call(
        product_kernel,
        model_width // half,
        [(normed, half_columns), (gate_low, whole((tokens, width)))],
        [((model_width, width), f32, rows_of(half, width))],
    )[0]
    grad_out = call(
        product_kernel,
        width // (2 * LANES),
        [(normed_out, pair_columns), (cot, whole((tokens, model_width)))],
        [((width, model_width), f32, rows_of(2 * LANES, model_width))],
    )[0]
    received, grad_z, grad_out = lax.optimization_barrier((received, grad_z, grad_out))
    grad_z, grad_out = lax.psum((grad_z, grad_out), ("dp", "seq"))
    later = call(
        functools.partial(scan_back_kernel, parts, ranges),
        1,
        [(received, whole((STATE, width))), (decays, whole((STATE, width)))],
        [((STATE, width), f32, whole((STATE, width)))],
    )[0]
    later = exchanged(later)

    def top(columns):
        return pl.BlockSpec((EDGE, columns), lambda i: (0, 0))

    last_rows = pl.BlockSpec((EDGE, LANES), lambda i: (tokens // EDGE - 1, 0))
    edge_grad = call(
        edge_kernel,
        1,
        [
            (later, whole((STATE, width))),
            (pre_x, top(width)),
            (pre_bc, top(bc_width)),
            (step, top(LANES)),
            (cumd, top(LANES)),
            (cumd, last_rows),
            (d_mixed, pl.BlockSpec((2 * EDGE, width), lambda i: (0, 0))),
            (d_values, top(width)),
            (d_bc, top(bc_width)),
            (small, small_spec),
        ],
        [((EDGE, width + bc_width), f32, whole((EDGE, width + bc_width)))],
    )[0]
    edge_next = from_behind(edge_grad, "seq", -1)

    def rows_before(columns):
        step_rows = CHUNK // EDGE
        return pl.BlockSpec(
            (EDGE, columns),
            lambda i: (jnp.maximum((chunks - 1 - i) * step_rows - 1, 0), 0),
        )

    x_low, own, send, bc_low, bc_rows, step_low, sums = call(
        finish_kernel,
        chunks,
        [
            (core_flag, flag_spec),
            (later, whole((STATE, width))),
            (full_starts, state_back),
            (pre_x, rows_back(width)),
            (pre_bc, rows_back(bc_width)),
            (inner_x, rows_back(width)),
            (inner_bc, rows_back(bc_width)),
            (inner_x, rows_before(width)),
            (inner_bc, rows_before(bc_width)),
            (edge, whole((EDGE, width + bc_width))),
            (edge_next, whole((EDGE, width + bc_width))),
            (step_raw, rows_back(LANES)),
            (step, rows_back(LANES)),
            (cumc, rows_back(LANES)),
            (cumd, rows_back(LANES)),
            (cumd, last_rows),
            (d_mixed, rows_back(width)),
            (d_values, rows_back(width)),
            (d_bc, rows_back(bc_width)),
            (d_step, rows_back(LANES)),
            (d_log, rows_back(LANES)),
            (conv_x, whole(conv_x.shape)),
            (conv_bc, whole(conv_bc.shape)),
            (small, small_spec),
            (col_out, whole((EDGE, width))),
        ],
        [
            ((tokens, width), bf16, rows_back(width)),
            ((tokens, half), bf16, rows_back(half)),
            ((tokens, half), f32, rows_back(half)),
            ((tokens, bc_width), bf16, rows_back(bc_width)),
            (
                (parts_head, bc_share, tokens),
                f32,
                pl.BlockSpec((parts_head, bc_share, CHUNK), lambda i: (0, 0, chunks - 1 - i)),
            ),
            ((tokens, LANES), bf16, rows_back(LANES)),
            ((EDGE, model_width), f32, whole((EDGE, model_width))),
        ],
        [
            pltpu.VMEM((CHUNK + EDGE, width), f32),
            pltpu.VMEM((CHUNK + EDGE, bc_width), f32),
            pltpu.VMEM((CHUNK + EDGE, width), f32),
            pltpu.VMEM((CHUNK + EDGE, bc_width), f32),
        ],
    )
    peer = swap_cores(send)
    blocks = model_width // half
    per = ranges // blocks
    x_rows, small_rows = model_width // ranges, half // ranges
    features = 2 * LANES
    feature_blocks = model_width // features
    by_features = pl.BlockSpec((tokens, features), lambda i: (0, i))
    both, parts_out = call(
        norm_back_kernel,
        feature_blocks,
        [
            (gate_low, whole((tokens, width))),
            (x_low, whole((tokens, width))),
            (bc_low, whole((tokens, bc_width))),
            (step_low, whole((tokens, LANES))),
            (normed_out, whole((tokens, width))),
            (hid, whole((tokens, model_width))),
            (hid, by_features),
            (norm_gain, pl.BlockSpec((features,), lambda i: (i,))),
            (w_z, rows_of(features, width)),
            (w_x, rows_of(features, width)),
            (w_bc, rows_of(features, bc_width)),
            (dt_rows, pl.BlockSpec((heads_here, features), lambda i: (0, i))),
            (w_out, pl.BlockSpec((width, features), lambda i: (0, i))),
            (sums, whole((EDGE, model_width))),
            (bc_rows, whole(bc_rows.shape)),
        ],
        [
            (
                (2, tokens, model_width),
                f32,
                pl.BlockSpec((2, tokens, features), lambda i: (0, 0, i)),
            ),
            (
                (parts_head, bc_share + EDGE, tokens),
                f32,
                whole((parts_head, bc_share + EDGE, tokens)),
            ),
        ],
        [
            pltpu.VMEM((tokens, LANES), f32),
            pltpu.VMEM((tokens, LANES), f32),
            pltpu.VMEM((EDGE, model_width), f32),
        ],
    )
    bc_parts = lax.all_to_all(parts_out, "head", 0, 0)
    shared = pl.BlockSpec((per, x_rows + small_rows, half), lambda i: (i, 0, 0))
    small_block = pl.BlockSpec((ranges, small_rows, half), lambda i: (0, x_rows // small_rows, 0))
    grad_x = call(
        outer_kernel,
        blocks,
        [
            (normed, half_columns),
            (own, whole((tokens, half))),
            (normed_peer, half_columns),
            (peer, whole((tokens, half))),
        ],
        [((ranges, x_rows + small_rows, half), f32, shared)],
    )[0]
    grad_x, bc_parts = lax.optimization_barrier((grad_x, bc_parts))
    grad_x, dots = call(
        share_kernel,
        1,
        [
            (grad_x, pl.BlockSpec(memory_space=pl.ANY)),
            (bc_parts, whole(bc_parts.shape)),
            (step_low, whole(step_low.shape)),
            (normed, whole(normed.shape)),
            (sums, whole(sums.shape)),
        ],
        [
            (grad_x.shape, f32, small_block),
            ((EDGE, tokens), f32, whole((EDGE, tokens))),
        ],
        aliases={0: 0},
    )
    row_dot = dots[6]
    branch_own, norm_own = lax.psum_scatter(both, "head", scatter_dimension=2, tiled=True)
    grad_x = lax.all_to_all(grad_x, "seq", 0, 0)
    lane_block = pl.BlockSpec(grad_x.shape[:2] + (LANES,), lambda i: (0, 0, i))
    grad_x = call(
        total_kernel, half // LANES, [(grad_x, lane_block)], [(grad_x.shape, f32, lane_block)]
    )[0]
    grad_x = lax.all_to_all(grad_x, "seq", 0, 0)
    grad_z = call(
        copy_kernel,
        blocks,
        [(grad_z, rows_of(half, width))],
        [((model_width, width), f32, rows_of(half, width))],
    )[0]
    grad_out = call(
        copy_kernel,
        blocks,
        [(grad_out, rows_of(half // 2, model_width))],
        [((width, model_width), f32, rows_of(half // 2, model_width))],
    )[0]
    branch_own, norm_own, grad_z, grad_out = lax.optimization_barrier(
        (branch_own, norm_own, grad_z, grad_out)
    )
    first = head_pos * share
    rows_own = lax.dynamic_slice_in_dim(hid, first, share, 1).astype(f32)
    output = (rows_own + branch_own).astype(bf16)[None]
    rows_all = hid.astype(f32)
    scale_in = lax.rsqrt(jnp.mean(rows_all * rows_all, axis=1, keepdims=True) + epsilon)
    gain_own = lax.dynamic_slice_in_dim(norm_gain, first, share, 0)
    cot_own = lax.dynamic_slice_in_dim(cot, first, share, 1).astype(f32)
    unit_own = rows_own * scale_in
    grad_in = scale_in * (norm_own * gain_own - unit_own * row_dot[:, None] / model_width)
    hidden_grad = (cot_own + grad_in).astype(bf16)[None]
    grad_x, grad_z, grad_out, output, hidden_grad = lax.optimization_barrier(
        (grad_x, grad_z, grad_out, output, hidden_grad)
    )
    x_peer = swap_cores(grad_x)
    grads = grad_x
    grad_x = call(
        join_kernel,
        blocks,
        [(core_flag, flag_spec), (grads, shared), (x_peer, shared)],
        [((model_width, width), f32, rows_of(half, width))],
    )[0]
    taps = conv_x.shape[0]
    shapes = [
        (bc_share, model_width),
        (heads_here, model_width),
        (taps, width),
        (taps, bc_width),
        (width,),
        (bc_width,),
        (width,),
        (share,),
        (EDGE, LANES),
    ]
    dealt = call(
        deal_kernel,
        1,
        [
            (grads, small_block),
            (x_peer, small_block),
        ],
        [(shape, f32, whole(shape)) for shape in shapes],
        [pltpu.VMEM((EDGE, model_width), f32)],
    )
    g_bc, g_dt, g_conv_x, g_conv_bc, g_bias_x, g_bias_bc, g_gain, g_norm, by_head = dealt
    return (
        output,
        hidden_grad,
        g_norm,
        grad_z,
        grad_x,
        g_bc.T,
        g_dt.T,
        g_conv_x,
        g_conv_bc,
        g_bias_x,
        g_bias_bc,
        by_head[1, :heads_here],
        by_head[0, :heads_here],
        by_head[2, :heads_here],
        g_gain,
        grad_out,
    )


def solution(mesh):
    placed = (
        P("dp", "seq", None),
        P("dp", "seq", None),
        P(),
        P(None, "head"),
        P(None, "head"),
        P(),
        P(None, "head"),
        P(None, "head"),
        P(),
        P("head"),
        P(),
        P("head"),
        P("head"),
        P("head"),
        P("head"),
        P("head", None),
    )
    return jax.shard_map(
        per_device,
        mesh=mesh,
        in_specs=placed,
        out_specs=(
            P("dp", "seq", "head"),
            P("dp", "seq", "head"),
            P("head"),
            P(None, "head"),
            P(None, "head"),
            P(None, "head"),
            P(None, "head"),
            P(None, "head"),
            P(),
            P("head"),
            P(),
            P("head"),
            P("head"),
            P("head"),
            P("head"),
            P("head", None),
        ),
        check_vma=False,
    )
```

```python
import functools

import jax
import jax.numpy as jnp
from jax import lax
from jax.experimental import pallas as pl
from jax.experimental.pallas import tpu as pltpu
from jax.sharding import PartitionSpec as P

HEADDIM = 64
STATE = 128
CHUNK = 128
LANES = 128
EDGE = 8

epsilon = 1e-05
f32 = jnp.float32
bf16 = jnp.bfloat16


def low(value):
    return value.astype(bf16)


def dot(left, right):
    return jnp.dot(left, right, preferred_element_type=f32)


def dot_nt(left, right):
    return lax.dot_general(left, right, (((1,), (1,)), ((), ())), preferred_element_type=f32)


def dot_tn(left, right):
    return lax.dot_general(left, right, (((0,), (0,)), ((), ())), preferred_element_type=f32)


def parts_of(value, count):
    terms = []
    for _ in range(count):
        term = value.astype(bf16)
        terms.append(term)
        value = value - term.astype(f32)
    return terms


def dot_split(left, right):
    high, rest = parts_of(right, 2)
    return dot(left, high) + dot(left, rest)


def head_map(width):
    head = lax.broadcasted_iota(jnp.int32, (LANES, width), 0)
    column = lax.broadcasted_iota(jnp.int32, (LANES, width), 1)
    return (lax.shift_right_logical(column, 6) == head).astype(f32).astype(bf16)


def spread(per_head, heads):
    high, rest = parts_of(per_head, 2)
    return dot(high, heads) + dot(rest, heads)


def per_head_sum(channels, heads):
    high, rest = parts_of(channels, 2)
    return dot_nt(high, heads) + dot_nt(rest, heads)


def running(mask, value):
    terms = parts_of(value, 3)
    return dot(mask, terms[0]) + dot(mask, terms[1]) + dot(mask, terms[2])


def as_row(vector):
    return vector[...].reshape(1, vector.shape[0])


def row_col():
    row = lax.broadcasted_iota(jnp.int32, (CHUNK, CHUNK), 0)
    column = lax.broadcasted_iota(jnp.int32, (CHUNK, CHUNK), 1)
    return row, column


def as_mask(where):
    return where.astype(f32).astype(bf16)


def sigmoid(value):
    return 1.0 / (1.0 + jnp.exp(-value))


def silu(value):
    return value * sigmoid(value)


def silu_slope(value):
    sigma = sigmoid(value)
    return sigma * (1.0 + value * (1.0 - sigma))


def softplus(value):
    return jnp.maximum(value, 0.0) + jnp.log1p(jnp.exp(-jnp.abs(value)))


def column_sum(value):
    return jnp.sum(value, axis=0, keepdims=True)


def row_sum(value):
    return jnp.sum(value, axis=1, keepdims=True)


def exp_below(where, value):
    return jnp.exp(jnp.where(where, value, -1e30))


def project_kernel(hid, gain, wx, wbc, wdt, normed, normed32, inx, inbc, sraw, edge):
    rows = hid[...].astype(f32)
    scale = lax.rsqrt(jnp.mean(rows * rows, axis=1, keepdims=True) + epsilon)
    value = low(rows * scale * as_row(gain))
    normed[...] = value
    normed32[...] = value.astype(f32)
    width = inx.shape[1]
    inx[...] = dot(value, wx[...])
    inbc[...] = dot(value, wbc[...])
    edge[:, :width] = inx[CHUNK - EDGE :, :]
    edge[:, width:] = inbc[CHUNK - EDGE :, :]
    sraw[...] = jnp.zeros(sraw.shape, f32)
    sraw[:, : wdt.shape[0]] = dot_nt(value, wdt[...])


def conv_rows(ext, taps, bias):
    total = as_row(bias) + taps[0:1, :] * ext[pl.ds(EDGE - 3, CHUNK), :]
    for k in range(1, 4):
        total = total + taps[k : k + 1, :] * ext[pl.ds(EDGE - 3 + k, CHUNK), :]
    return total


def front_kernel(
    edge, inx, inbc, sraw, cx, cbc, bx, bbc, small,
    prex, prebc, step_out, cumc_out, cumd_out, starts, payload,
    extx, extbc, state, base,
):
    i = pl.program_id(0)
    width = inx.shape[1]

    @pl.when(i == 0)
    def _():
        extx[0:EDGE, :] = edge[:, :width]
        extbc[0:EDGE, :] = edge[:, width:]
        state[...] = jnp.zeros(state.shape, f32)
        base[...] = jnp.zeros(base.shape, f32)

    @pl.when(i > 0)
    def _():
        extx[0:EDGE, :] = extx[CHUNK : CHUNK + EDGE, :]
        extbc[0:EDGE, :] = extbc[CHUNK : CHUNK + EDGE, :]

    extx[EDGE:, :] = inx[...]
    extbc[EDGE:, :] = inbc[...]
    pre_x = conv_rows(extx, cx, bx)
    pre_bc = conv_rows(extbc, cbc, bbc)
    prex[...] = pre_x
    prebc[...] = pre_bc
    values = low(silu(pre_x)).astype(f32)
    keys_t = jnp.transpose(low(silu(pre_bc[:, :STATE])).astype(f32))
    step = softplus(sraw[...] + small[0:1, :])
    decay = -jnp.exp(small[1:2, :]) * step
    row, column = row_col()
    cumc = running(as_mask(row >= column), decay)
    last = cumc[CHUNK - 1 : CHUNK, :]
    step_out[...] = step
    cumc_out[...] = cumc
    cumd_out[...] = cumc + base[0:1, :]
    starts[0] = state[...]
    heads = head_map(width)
    weights = spread(jnp.exp(last - cumc) * step, heads)
    keep = spread(jnp.exp(jnp.broadcast_to(last, (EDGE, LANES))), heads)[0:1, :]
    state[...] = keep * state[...] + dot_split(low(keys_t), values * weights)
    base[...] = base[...] + last

    @pl.when(i == pl.num_programs(0) - 1)
    def _():
        payload[:, :width] = state[...]
        payload[:, width:] = jnp.broadcast_to(base[0:1, :], (STATE, LANES))


def scan_kernel(parts, ranges, received, incoming, decays):
    width = incoming.shape[1]
    decays[...] = spread(jnp.exp(received[:, width:]), head_map(width))
    carry = jnp.zeros((parts, width), f32)
    for i in range(ranges):
        here = slice(i * parts, (i + 1) * parts)
        incoming[here, :] = carry
        carry = decays[here, :] * carry + received[here, :width]


def scan_back_kernel(parts, ranges, received, decays, incoming):
    carry = jnp.zeros((parts, incoming.shape[1]), f32)
    for i in reversed(range(ranges)):
        here = slice(i * parts, (i + 1) * parts)
        incoming[here, :] = carry
        carry = decays[here, :] * carry + received[here, :]


def within_kernel(prex, prebc, step_in, cumc_in, starts, small, out):
    width = prex.shape[1]
    heads = head_map(width)
    act_x = silu(prex[...])
    values = low(act_x).astype(f32)
    act_bc = low(silu(prebc[...]))
    keys, reads = act_bc[:, :STATE], act_bc[:, STATE:]
    step, cumc = step_in[...], cumc_in[...]
    cum_t, step_t = jnp.transpose(cumc), jnp.transpose(step)
    carried = spread(jnp.exp(cumc), heads) * dot_split(reads, starts[0])
    carried = carried + spread(small[...], heads)[2:3, :] * act_x
    scores = dot_nt(reads, keys)
    row, column = row_col()
    causal = row >= column
    first = lax.broadcasted_iota(jnp.int32, (CHUNK, LANES), 1) < HEADDIM
    for pair in range(width // LANES):
        lanes = slice(pair * LANES, (pair + 1) * LANES)
        pieces, rests = [], []
        for h in (2 * pair, 2 * pair + 1):
            decayed = exp_below(causal, cumc[:, h : h + 1] - cum_t[h : h + 1, :])
            high, rest = parts_of(decayed * scores * step_t[h : h + 1, :], 2)
            pieces.append(high)
            rests.append(rest)
        here = values[:, lanes]
        halves = [low(jnp.where(first, here, 0.0)), low(jnp.where(first, 0.0, here))]
        mixing = jnp.concatenate(pieces + rests, axis=1)
        out[:, lanes] = carried[:, lanes] + dot(mixing, jnp.concatenate(halves * 2, axis=0))


def mix_kernel(incoming, pre_reads, cumd, within, gate_z, d_out, gain, mixed_out, sums):
    heads = head_map(within.shape[1])
    reads = low(silu(pre_reads[...]))
    mixed = within[...] + spread(jnp.exp(cumd[...]), heads) * dot_split(reads, incoming[...])
    mixed_out[...] = mixed
    gated = mixed * silu(gate_z[...])
    squares = row_sum(gated * gated)
    products = row_sum(d_out[...] * as_row(gain) * gated)
    column = lax.broadcasted_iota(jnp.int32, (CHUNK, LANES), 1)
    both = jnp.where(column == 0, squares, jnp.where(column == 1, products, 0.0))
    sums[...] = jnp.transpose(both)[0:2, :]


def gate_kernel(
    inner_all, totals, second, third, fourth, mixed_in, gate_z, d_out, pre_reads, cumd, gain,
    normed_out, gate_low, d_mixed, col_out, payload,
):
    i = pl.program_id(0)
    width = mixed_in.shape[1]
    heads = head_map(width)

    @pl.when(i == 0)
    def _():
        col_out[...] = jnp.zeros(col_out.shape, f32)
        payload[...] = jnp.zeros(payload.shape, f32)

    all_sums = (totals[...] + second[...]) + (third[...] + fourth[...])
    squares, products = (
        jnp.transpose(jnp.broadcast_to(all_sums[r : r + 1, :], (CHUNK, CHUNK)))[:, 0:1]
        for r in range(2)
    )
    scale = lax.rsqrt(squares / inner_all + epsilon)
    mean_dot = scale * products / inner_all
    gate = gate_z[...]
    sigma = sigmoid(gate)
    silu_z = gate * sigma
    mixed = mixed_in[...]
    unit = mixed * silu_z * scale
    d_normed = d_out[...]
    gain_row = as_row(gain)
    out_low = low(unit * gain_row)
    normed_out[...] = out_low
    d_gated = scale * (d_normed * gain_row - unit * mean_dot)
    g_low = low(d_gated * silu_z)
    d_mixed[...] = g_low
    slope = sigma * (1.0 + gate * (1.0 - sigma))
    gate_grad = low(d_gated * mixed * slope)
    gate_low[...] = gate_grad
    g = g_low.astype(f32)
    col_out[0:1, :] += column_sum(d_normed * unit)
    reads_t = jnp.transpose(low(silu(pre_reads[...])).astype(f32))
    payload[...] += dot_split(low(reads_t), g * spread(jnp.exp(cumd[...]), heads))


def back_kernel(
    prex, prebc, step_in, cumc_in, cumd, starts, incoming, d_mixed,
    d_values, d_bc, d_step, d_log,
    later, gy_t,
):
    i = pl.program_id(0)
    width = prex.shape[1]
    heads = head_map(width)

    @pl.when(i == 0)
    def _():
        later[...] = jnp.zeros(later.shape, f32)
        gy_t[...] = jnp.zeros(gy_t.shape, f32)

    values_low = low(silu(prex[...]))
    values = values_low.astype(f32)
    act_bc = low(silu(prebc[...]))
    keys, reads = act_bc[:, :STATE], act_bc[:, STATE:]
    step, cumc = step_in[...], cumc_in[...]
    cum_t = jnp.transpose(cumc)
    last = cumc[CHUNK - 1 : CHUNK, :]
    before = cumd[CHUNK - 1 : CHUNK, :] - last
    tops = jnp.concatenate(
        [jnp.broadcast_to(before, (EDGE, LANES)), jnp.broadcast_to(last, (EDGE, LANES))], axis=0
    )
    tops = spread(jnp.exp(tops), heads)
    start = starts[0] + tops[0:1, :] * incoming[...]
    keep = tops[EDGE : EDGE + 1, :]
    start_low, start_rest = parts_of(start, 2)
    step_wide = spread(step, heads)
    out_wide = spread(jnp.exp(last - cumc), heads)
    g_low = d_mixed[...]
    g = g_low.astype(f32)
    g_in = g * spread(jnp.exp(cumc), heads)
    g_in_low, g_in_rest = parts_of(g_in, 2)

    row, column = row_col()
    causal = row <= column
    scores_t = dot_nt(keys, reads)
    first = lax.broadcasted_iota(jnp.int32, (CHUNK, LANES), 1) < HEADDIM
    d_scores_t = jnp.zeros((CHUNK, CHUNK), f32)
    step_within = jnp.zeros((CHUNK, LANES), f32)
    later_low = low(later[...])
    onward = out_wide * dot(keys, later_low)
    for pair in range(width // LANES):
        lanes = slice(pair * LANES, (pair + 1) * LANES)
        g_pair = g[:, lanes]
        halves = (low(jnp.where(first, g_pair, 0.0)), low(jnp.where(first, 0.0, g_pair)))
        pieces = []
        for h, g_half in zip((2 * pair, 2 * pair + 1), halves):
            decayed = exp_below(causal, cum_t[h : h + 1, :] - cumc[:, h : h + 1])
            d_mixing = dot_nt(values_low[:, lanes], g_half)
            weighted = decayed * d_mixing
            step_col = step[:, h : h + 1]
            d_scores_t = d_scores_t + weighted * step_col
            product = weighted * scores_t
            step_within = step_within + jnp.where(column == h, row_sum(product), 0.0)
            gy_t[h : h + 1, :] = column_sum(product * step_col)
            pieces.append(low(decayed * scores_t))
        d_pair = dot(jnp.concatenate(pieces, axis=1), jnp.concatenate(halves, axis=0))
        d_values[:, lanes] = step_wide[:, lanes] * (d_pair + onward[:, lanes])

    d_keys = dot(low(d_scores_t), reads) + dot_nt(low(values * step_wide * out_wide), later_low)
    d_reads = dot(low(jnp.transpose(d_scores_t)), keys) + dot_nt(g_in_low, start_low)
    d_reads = d_reads + dot_nt(g_in_low, start_rest) + dot_nt(g_in_rest, start_low)
    d_bc[:, :STATE] = d_keys
    d_bc[:, STATE:] = d_reads
    from_start = dot(reads, start_low) + dot(reads, start_rest)
    from_start = per_head_sum(g_in * from_start, heads)
    step_onward = per_head_sum(values * onward, heads)
    d_step[...] = step_within + step_onward
    across = column_sum(start * later[...])
    across = per_head_sum(jnp.broadcast_to(across, (EDGE, width)), heads)[0:1, :] * jnp.exp(last)
    inside = jnp.transpose(gy_t[...]) - step * step_within + from_start
    d_log[...] = (
        running(as_mask(row <= column), inside)
        + running(as_mask(row > column), step * step_onward)
        + across
    )
    later[...] = keep * later[...] + dot(low(jnp.transpose(reads.astype(f32))), g_in_low)


def edge_kernel(incoming, prex, prebc, step_in, cumd, total, d_mixed, d_values, d_bc, small, out):
    width = prex.shape[1]
    heads = head_map(width)
    low_in = low(incoming[...])
    act_bc = low(silu(prebc[...]))
    step = step_in[...]
    weight = spread(step * jnp.exp(total[EDGE - 1 : EDGE, :] - cumd[...]), heads)
    skip = spread(small[...], heads)[2:3, :]
    values = low(silu(prex[...])).astype(f32)
    d_val = d_values[...] + weight * dot(act_bc[:, :STATE], low_in)
    d_keys = d_bc[:, :STATE] + dot_nt(low(values * weight), low_in)
    d_act = d_val + skip * d_mixed[...].astype(f32)[:EDGE]
    out[:, :width] = d_act * silu_slope(prex[...])
    out[:, width : width + STATE] = d_keys * silu_slope(prebc[:, :STATE])
    out[:, width + STATE :] = d_bc[:, STATE:] * silu_slope(prebc[:, STATE:])


def conv_back(chunk, ext, inner, before, edge, taps, d_pre, sums, columns):
    ext[0:CHUNK, :] = d_pre
    d_inner = taps[3:4, :] * d_pre
    for k in range(3):
        d_inner = d_inner + taps[k : k + 1, :] * ext[pl.ds(3 - k, CHUNK), :]
    ext[CHUNK:, :] = ext[0:EDGE, :]
    rows = jnp.where(chunk == 0, edge, before[...])
    inner[0:EDGE, :] = rows
    for k in range(4):
        sums[k : k + 1, columns] += column_sum(d_pre * inner[pl.ds(EDGE - 3 + k, CHUNK), :])
    sums[4:5, columns] += column_sum(d_pre)
    return d_inner


def finish_kernel(
    core, incoming, starts, early, prex, prebc, inx, inbc, before_x, before_bc, edge, edge_next,
    sraw, step_in, cumc_in, cumd_in, total, d_mixed, d_values, d_bc, d_step, d_log, cx, cbc, small,
    col_in,
    x_low, own, send, bc_low, bc_rows, step_out, sums,
    ext_x, ext_bc, inner_x, inner_bc,
):
    i = pl.program_id(0)
    chunk = pl.num_programs(0) - 1 - i
    width = prex.shape[1]
    half = width // 2
    heads = head_map(width)

    @pl.when(i == 0)
    def _():
        ext_x[CHUNK:, :] = edge_next[:, :width]
        ext_bc[CHUNK:, :] = edge_next[:, width:]
        sums[...] = jnp.zeros(sums.shape, f32)
        sums[5:6, :width] = col_in[0:1, :]

    late = incoming[...]
    late_low = low(late)
    act_bc = low(silu(prebc[...]))
    keys = act_bc[:, :STATE]
    pre_x = prex[...]
    sigma = sigmoid(pre_x)
    slope_x = sigma * (1.0 + pre_x * (1.0 - sigma))
    values = low(pre_x * sigma).astype(f32)
    step, cumd = step_in[...], cumd_in[...]
    end = total[EDGE - 1 : EDGE, :]
    step_wide = spread(step, heads)
    out_wide = spread(jnp.exp(end - cumd), heads)
    skip = spread(small[...], heads)[2:3, :]
    onward = out_wide * dot(keys, late_low)
    d_val = d_values[...] + step_wide * onward
    d_keys = d_bc[:, :STATE] + dot_nt(low(values * step_wide * out_wide), late_low)
    step_onward = per_head_sum(values * onward, heads)
    before = cumd[CHUNK - 1 : CHUNK, :] - cumc_in[CHUNK - 1 : CHUNK, :]
    tops = spread(jnp.exp(jnp.broadcast_to(before, (EDGE, LANES))), heads)[0:1, :]
    across = column_sum((starts[0] + tops * early[...]) * late)
    across = per_head_sum(jnp.broadcast_to(across, (EDGE, width)), heads)[0:1, :]
    row, column = row_col()
    log_grad = (
        d_log[...]
        + running(as_mask(row > column), step * step_onward)
        + across * jnp.exp(end - before)
    )
    rate = jnp.exp(small[1:2, :])
    step_grad = d_step[...] + step_onward - rate * log_grad
    raw = sraw[...] + small[0:1, :]
    step_pre = step_grad * sigmoid(raw)
    for_heads = slice(width + 2 * STATE, width + 2 * STATE + LANES)
    sums[0:1, for_heads] += column_sum(log_grad * (-rate * step))
    sums[1:2, for_heads] += column_sum(step_pre)
    step_out[...] = low(step_pre)

    g = d_mixed[...].astype(f32)
    sums[6:7, :width] += column_sum(g * (pre_x * sigma))
    d_pre_x = (d_val + skip * g) * slope_x
    inner_x[EDGE:, :] = inx[...]
    of_x = slice(0, width)
    d_in = low(
        conv_back(chunk, ext_x, inner_x, before_x, edge[:, of_x], cx, d_pre_x, sums, of_x)
    )
    x_low[...] = d_in
    wide = d_in.astype(f32)
    is_first = core[0] == 0
    own[...] = low(jnp.where(is_first, wide[:, :half], wide[:, half:]))
    send[...] = jnp.where(is_first, wide[:, half:], wide[:, :half])

    d_act_bc = jnp.concatenate([d_keys, d_bc[:, STATE:]], axis=1)
    d_pre_bc = d_act_bc * silu_slope(prebc[...])
    inner_bc[EDGE:, :] = inbc[...]
    of_bc = slice(width, width + 2 * STATE)
    d_in = conv_back(
        chunk, ext_bc, inner_bc, before_bc, edge[:, of_bc], cbc, d_pre_bc, sums, of_bc
    )
    bc_low[...] = low(d_in)
    shares = jnp.transpose(d_in)
    share = bc_rows.shape[1] - 2 * EDGE
    for k in range(bc_rows.shape[0]):
        bc_rows[k, :share, :] = shares[k * share : (k + 1) * share, :]
        bc_rows[k, share:, :] = jnp.zeros((2 * EDGE, CHUNK), f32)

    @pl.when(chunk == 0)
    def _():
        for row_at in range(5):
            for j in range(2):
                at = width + j * STATE
                line = sums[row_at : row_at + 1, at : at + STATE]
                to = share + 2 * row_at + j
                for k in range(bc_rows.shape[0]):
                    bc_rows[k, to : to + 1, :] = line


def norm_back_kernel(
    buffer, dg, dx, dbc, dst, hid, gain, wz, wx, wbc, wdt, out, dots, scale, along
):
    i = pl.program_id(0)
    _, count, width = out.shape

    @pl.when(i == 0)
    def _():
        rows = hid[...].astype(f32)
        mean = jnp.mean(rows * rows, axis=1, keepdims=True)
        scale[...] = jnp.broadcast_to(lax.rsqrt(mean + epsilon), scale.shape)
        along[...] = jnp.zeros(along.shape, f32)

    total = dot_nt(dg[...], wz[...]) + dot_nt(dx[...], wx[...])
    total = total + dot_nt(dbc[...], wbc[...])
    total = total + dot(dst[:, : wdt.shape[0]], wdt[...])
    out[0] = total
    here = pl.ds(pl.multiple_of(i * width, width), width)
    weighted = total * (hid[:, here].astype(f32) * scale[:, 0:1]) * as_row(gain)
    partial = weighted[:, :LANES]
    for k in range(1, width // LANES):
        partial = partial + weighted[:, k * LANES : (k + 1) * LANES]
    along[...] += partial

    @pl.when(i == pl.num_programs(0) - 1)
    def _():
        for j in range(count // CHUNK):
            lanes = slice(j * CHUNK, (j + 1) * CHUNK)
            line = column_sum(jnp.transpose(along[lanes, :]))
            dots[:, lanes] = jnp.broadcast_to(line, (EDGE, CHUNK))


def share_kernel(
    buffer, parts, step_low, normed, sums, gains_z, gains_x, gain, wbc_rows, wdt, out
):
    share = parts[0]
    for k in range(1, parts.shape[0]):
        share = share + parts[k]
    count = share.shape[0] - 2 * EDGE
    extra = share[count:, :STATE]
    features = normed.shape[1]
    width = features // 2
    pairs = [
        jnp.concatenate([extra[2 * r : 2 * r + 1, :], extra[2 * r + 1 : 2 * r + 2, :]], axis=1)
        for r in range(EDGE)
    ]
    summed = jnp.concatenate(
        [
            jnp.zeros((EDGE, width), f32),
            jnp.concatenate(pairs, axis=0),
            jnp.zeros((EDGE, features - width - 2 * STATE), f32),
        ],
        axis=1,
    )
    steps = 2 * EDGE
    of_w = dot(low(share[:count, :]), normed[...])
    of_dt = dot_tn(step_low[...], normed[...])[:steps, :]
    heads = wdt.shape[0]
    gains = gains_z[0:1, :] + gains_x[0:1, :] + column_sum(of_w * wbc_rows[...].astype(f32))
    gains = gains + column_sum(of_dt[:heads, :] * wdt[...].astype(f32))
    gains = gains / as_row(gain)
    lane = lax.broadcasted_iota(jnp.int32, (EDGE, features), 1)
    row = lax.broadcasted_iota(jnp.int32, (EDGE, features), 0)
    of_bc = (lane >= width) & (lane < width + 2 * STATE) & (row < 5)
    tiny = jnp.where(row == 7, gains, jnp.where(of_bc, summed, sums[...]))
    ranges, rows, half = out.shape
    spare = jnp.zeros((rows * ranges * half // features - count - steps - EDGE, features), f32)
    stacked = jnp.concatenate([of_w, of_dt, tiny, spare], axis=0)
    blocks = features // half
    per = ranges // blocks
    for k in range(blocks):
        out[k * per : (k + 1) * per] = stacked[:, k * half : (k + 1) * half].reshape(per, rows, half)


def place_kernel(core, blocks, out):
    out[...] = blocks[:, : out.shape[0] // blocks.shape[0], :].reshape(out.shape)


def deal_kernel(
    core, blocks, mine, theirs, onto,
    out, bc, dt, conv_x, conv_bc, bias_x, bias_bc, gain, dt_bias, a_log, skip, sums,
):
    out[...] = blocks[:, : out.shape[0] // blocks.shape[0], :].reshape(out.shape)

    @pl.when(pl.program_id(0) == 0)
    def _():
        share, steps = bc.shape[0], dt.shape[0]
        taps, width = conv_x.shape
        bc_width = conv_bc.shape[1]
        total = mine[...] + theirs[...]
        ranges, count, half = total.shape
        per = ranges // (bc.shape[1] // half)
        first = share + 2 * EDGE
        for k in range(bc.shape[1] // half):
            lanes = slice(k * half, (k + 1) * half)
            block = total[k * per : (k + 1) * per].reshape(per * count, half)
            bc[:, lanes] = block[:share, :]
            dt[:, lanes] = block[share : share + steps, :]
            sums[:, lanes] = block[first : first + EDGE, :]
        conv_x[...] = sums[:taps, :width]
        bias_x[...] = sums[taps, :width]
        conv_bc[...] = sums[:taps, width : width + bc_width]
        bias_bc[...] = sums[taps, width : width + bc_width]
        gain[...] = sums[5, :width]
        at = width + bc_width
        a_log[...] = sums[0, at : at + steps]
        dt_bias[...] = sums[1, at : at + steps]
        skip[...] = per_head_sum(sums[:, :width], head_map(width))[6, :steps]


def along_rows(value):
    ones = jnp.ones((EDGE, value.shape[1]), bf16)
    high, rest = parts_of(value, 2)
    return dot_nt(ones, high) + dot_nt(ones, rest)


def early_kernel(normed, gate_grad, w_z, normed_out, cot, z_out, out_out, gains):
    product = dot_tn(normed[...], gate_grad[...])
    z_out[...] = product
    gains[...] = along_rows(product * w_z[...].astype(f32))
    out_out[...] = dot_tn(normed_out[...], cot[...])


def branch_kernel(left, right, out):
    out[0] = dot(left[...], right[...])


def round_kernel(source, out):
    out[...] = low(source[...])


def outer_kernel(core, left, right, left_peer, right_peer, weight, out, gains):
    product = dot_tn(left[...], right[...]) + dot_tn(left_peer[...], low(right_peer[...]))
    per, _, half = out.shape
    count = product.shape[0] // per
    out[:, :count, :] = product.reshape(per, count, half)
    lower, upper = weight[:, :half].astype(f32), weight[:, half:].astype(f32)
    gains[...] = along_rows(product * jnp.where(core[0] == 0, lower, upper))


def total_kernel(parts, out):
    total = parts[0]
    for k in range(1, parts.shape[0]):
        total = total + parts[k]
    out[...] = jnp.broadcast_to(total[None], out.shape)


def whole(shape):
    return pl.BlockSpec(shape, lambda i: (0,) * len(shape))


def call(kernel, grid, ins, outs, scratch=(), flops=0, moved=0, megabytes=58, aliases=None):
    return pl.pallas_call(
        kernel,
        grid=(grid,),
        in_specs=[spec for _, spec in ins],
        out_specs=[spec for _, _, spec in outs],
        out_shape=[jax.ShapeDtypeStruct(shape, kind) for shape, kind, _ in outs],
        scratch_shapes=list(scratch),
        input_output_aliases=aliases or {},
        compiler_params=pltpu.CompilerParams(
            dimension_semantics=("arbitrary",), vmem_limit_bytes=megabytes * 2**20
        ),
        cost_estimate=pl.CostEstimate(flops=flops, bytes_accessed=moved, transcendentals=0),
    )(*[array for array, _ in ins])


def from_behind(shard, axis, by):
    peers = lax.axis_size(axis)
    pairs = [(i, i + by) for i in range(peers) if 0 <= i + by < peers]
    return lax.ppermute(shard, axis, pairs)


def swap_cores(shard):
    return lax.ppermute(shard, "dp", [(0, 1), (1, 0)])


def per_device(
    hidden,
    cotangent,
    norm_gain,
    w_z,
    w_x,
    w_bc,
    w_dt,
    conv_x,
    conv_bc,
    bias_x,
    bias_bc,
    dt_bias,
    a_log,
    skip_d,
    gain_out,
    w_out,
):
    hid, cot = hidden[0], cotangent[0]
    tokens, model_width = hid.shape
    heads_here = w_dt.shape[1]
    width = w_z.shape[1]
    half = width // 2
    bc_width = w_bc.shape[1]
    parts_head = lax.axis_size("head")
    bc_share = bc_width // parts_head
    chunks = tokens // CHUNK
    ranges = lax.axis_size("seq")
    parts = STATE // ranges
    head_pos = lax.axis_index("head")
    core = lax.axis_index("dp").astype(jnp.int32)
    core_flag = core.reshape(1)
    flag_spec = pl.BlockSpec(memory_space=pltpu.SMEM)

    def rows_of(count, columns):
        return pl.BlockSpec((count, columns), lambda i: (i, 0))

    def rows(columns):
        return rows_of(CHUNK, columns)

    def rows_back(columns):
        return pl.BlockSpec((CHUNK, columns), lambda i: (chunks - 1 - i, 0))

    pair_line = pl.BlockSpec((2, CHUNK), lambda i: (0, i))
    state_spec = pl.BlockSpec((1, STATE, width), lambda i: (i, 0, 0))
    state_back = pl.BlockSpec((1, STATE, width), lambda i: (chunks - 1 - i, 0, 0))
    dt_rows = w_dt.T
    bc_own_rows = lax.dynamic_slice_in_dim(w_bc, head_pos * bc_share, bc_share, 1).T
    small = jnp.pad(
        jnp.stack([dt_bias, a_log, skip_d]), ((0, EDGE - 3), (0, LANES - heads_here))
    )
    small_spec = whole((EDGE, LANES))

    normed, normed32, inner_x, inner_bc, step_raw, edge = call(
        project_kernel,
        chunks,
        [
            (hid, rows(model_width)),
            (norm_gain, whole((model_width,))),
            (w_x, whole(w_x.shape)),
            (w_bc, whole(w_bc.shape)),
            (dt_rows, whole(dt_rows.shape)),
        ],
        [
            ((tokens, model_width), bf16, rows(model_width)),
            ((tokens, model_width), f32, rows(model_width)),
            ((tokens, width), f32, rows(width)),
            ((tokens, bc_width), f32, rows(bc_width)),
            ((tokens, LANES), f32, rows(LANES)),
            ((EDGE, width + bc_width), f32, whole((EDGE, width + bc_width))),
        ],
        flops=2 * tokens * model_width * (width + bc_width),
        moved=18 << 20,
    )
    edge = from_behind(edge, "seq", 1)
    gate_z = jnp.dot(normed, w_z, preferred_element_type=f32)
    d_out = jnp.einsum("td,id->ti", cot, w_out, preferred_element_type=f32)
    normed_peer = swap_cores(normed32)

    pre_x, pre_bc, step, cumc, cumd, starts, payload = call(
        front_kernel,
        chunks,
        [
            (edge, whole((EDGE, width + bc_width))),
            (inner_x, rows(width)),
            (inner_bc, rows(bc_width)),
            (step_raw, rows(LANES)),
            (conv_x, whole(conv_x.shape)),
            (conv_bc, whole(conv_bc.shape)),
            (bias_x, whole((width,))),
            (bias_bc, whole((bc_width,))),
            (small, small_spec),
        ],
        [
            ((tokens, width), f32, rows(width)),
            ((tokens, bc_width), f32, rows(bc_width)),
            ((tokens, LANES), f32, rows(LANES)),
            ((tokens, LANES), f32, rows(LANES)),
            ((tokens, LANES), f32, rows(LANES)),
            ((chunks, STATE, width), f32, state_spec),
            ((STATE, width + LANES), f32, whole((STATE, width + LANES))),
        ],
        [
            pltpu.VMEM((CHUNK + EDGE, width), f32),
            pltpu.VMEM((CHUNK + EDGE, bc_width), f32),
            pltpu.VMEM((STATE, width), f32),
            pltpu.VMEM((EDGE, LANES), f32),
        ],
        flops=2 * tokens * STATE * width,
        moved=8 << 20,
    )

    def exchanged(array):
        blocks = array.reshape(ranges, parts, array.shape[1])
        return lax.all_to_all(blocks, "seq", 0, 0).reshape(array.shape)

    normed_peer = call(
        round_kernel,
        chunks,
        [(normed_peer, rows(model_width))],
        [((tokens, model_width), bf16, rows(model_width))],
    )[0]
    rows_all = hid.astype(f32)
    scale_in = lax.rsqrt(jnp.mean(rows_all * rows_all, axis=1, keepdims=True) + epsilon)
    received, normed_peer, bc_own_rows = lax.optimization_barrier(
        (exchanged(payload), normed_peer, bc_own_rows)
    )
    within = call(
        within_kernel,
        chunks,
        [
            (pre_x, rows(width)),
            (pre_bc, rows(bc_width)),
            (step, rows(LANES)),
            (cumc, rows(LANES)),
            (starts, state_spec),
            (small, small_spec),
        ],
        [((tokens, width), f32, rows(width))],
        flops=6 * tokens * CHUNK * width,
        moved=8 << 20,
    )[0]
    incoming, decays = call(
        functools.partial(scan_kernel, parts, ranges),
        1,
        [(received, whole(received.shape))],
        [((STATE, width), f32, whole((STATE, width)))] * 2,
        moved=1 << 20,
    )
    incoming = exchanged(incoming)

    reads_rows = pl.BlockSpec((CHUNK, STATE), lambda i: (i, 1))
    mixed, sums = call(
        mix_kernel,
        chunks,
        [
            (incoming, whole((STATE, width))),
            (pre_bc, reads_rows),
            (cumd, rows(LANES)),
            (within, rows(width)),
            (gate_z, rows(width)),
            (d_out, rows(width)),
            (gain_out, whole((width,))),
        ],
        [((tokens, width), f32, rows(width)), ((2, tokens), f32, pair_line)],
        flops=2 * tokens * STATE * width,
        moved=10 << 20,
    )
    totals = [sums]
    for by in range(1, parts_head):
        pairs = [(i, (i + by) % parts_head) for i in range(parts_head)]
        totals.append(lax.ppermute(sums, "head", pairs))
    normed_out, gate_low, d_mixed, col_out, payload = call(
        functools.partial(gate_kernel, width * parts_head),
        chunks,
        [
            *[(line, pair_line) for line in totals],
            (mixed, rows(width)),
            (gate_z, rows(width)),
            (d_out, rows(width)),
            (pre_bc, reads_rows),
            (cumd, rows(LANES)),
            (gain_out, whole((width,))),
        ],
        [
            ((tokens, width), bf16, rows(width)),
            ((tokens, width), bf16, rows(width)),
            ((tokens, width), bf16, rows(width)),
            ((EDGE, width), f32, whole((EDGE, width))),
            ((STATE, width), f32, whole((STATE, width))),
        ],
        flops=2 * tokens * STATE * width,
        moved=14 << 20,
    )

    received = exchanged(payload)
    share = model_width // parts_head
    d_values, d_bc, d_step, d_log = call(
        back_kernel,
        chunks,
        [
            (pre_x, rows_back(width)),
            (pre_bc, rows_back(bc_width)),
            (step, rows_back(LANES)),
            (cumc, rows_back(LANES)),
            (cumd, rows_back(LANES)),
            (starts, state_back),
            (incoming, whole((STATE, width))),
            (d_mixed, rows_back(width)),
        ],
        [
            ((tokens, width), f32, rows_back(width)),
            ((tokens, bc_width), f32, rows_back(bc_width)),
            ((tokens, LANES), f32, rows_back(LANES)),
            ((tokens, LANES), f32, rows_back(LANES)),
        ],
        [pltpu.VMEM((STATE, width), f32), pltpu.VMEM((LANES, CHUNK), f32)],
    )
    half_columns = pl.BlockSpec((tokens, half), lambda i: (0, i))
    gain_block = pl.BlockSpec((EDGE, half), lambda i: (0, i))
    grad_z, grad_out, gains_z = call(
        early_kernel,
        model_width // (2 * LANES),
        [
            (normed, pl.BlockSpec((tokens, 2 * LANES), lambda i: (0, i))),
            (gate_low, whole((tokens, width))),
            (w_z, rows_of(2 * LANES, width)),
            (normed_out, pl.BlockSpec((tokens, LANES), lambda i: (0, i))),
            (cot, whole((tokens, model_width))),
        ],
        [
            ((model_width, width), f32, rows_of(2 * LANES, width)),
            ((width, model_width), f32, rows_of(LANES, model_width)),
            ((EDGE, model_width), f32, pl.BlockSpec((EDGE, 2 * LANES), lambda i: (0, i))),
        ],
    )
    received, grad_z, grad_out = lax.optimization_barrier((received, grad_z, grad_out))
    grad_z, grad_out = lax.psum((grad_z, grad_out), ("dp", "seq"))
    later = call(
        functools.partial(scan_back_kernel, parts, ranges),
        1,
        [(received, whole((STATE, width))), (decays, whole((STATE, width)))],
        [((STATE, width), f32, whole((STATE, width)))],
    )[0]
    later = exchanged(later)

    def top(columns):
        return pl.BlockSpec((EDGE, columns), lambda i: (0, 0))

    last_rows = pl.BlockSpec((EDGE, LANES), lambda i: (tokens // EDGE - 1, 0))
    edge_grad = call(
        edge_kernel,
        1,
        [
            (later, whole((STATE, width))),
            (pre_x, top(width)),
            (pre_bc, top(bc_width)),
            (step, top(LANES)),
            (cumd, top(LANES)),
            (cumd, last_rows),
            (d_mixed, pl.BlockSpec((2 * EDGE, width), lambda i: (0, 0))),
            (d_values, top(width)),
            (d_bc, top(bc_width)),
            (small, small_spec),
        ],
        [((EDGE, width + bc_width), f32, whole((EDGE, width + bc_width)))],
    )[0]
    branch = call(
        branch_kernel,
        3,
        [
            (normed_out, whole((tokens, width))),
            (w_out, pl.BlockSpec((width, 4 * LANES), lambda i: (0, i))),
        ],
        [
            (
                (2, tokens, model_width),
                f32,
                pl.BlockSpec((1, tokens, 4 * LANES), lambda i: (0, 0, i)),
            )
        ],
    )[0]
    edge_next, branch = lax.optimization_barrier((from_behind(edge_grad, "seq", -1), branch))

    def rows_before(columns):
        step_rows = CHUNK // EDGE
        return pl.BlockSpec(
            (EDGE, columns),
            lambda i: (jnp.maximum((chunks - 1 - i) * step_rows - 1, 0), 0),
        )

    x_low, own, send, bc_low, bc_rows, step_low, sums = call(
        finish_kernel,
        chunks,
        [
            (core_flag, flag_spec),
            (later, whole((STATE, width))),
            (starts, state_back),
            (incoming, whole((STATE, width))),
            (pre_x, rows_back(width)),
            (pre_bc, rows_back(bc_width)),
            (inner_x, rows_back(width)),
            (inner_bc, rows_back(bc_width)),
            (inner_x, rows_before(width)),
            (inner_bc, rows_before(bc_width)),
            (edge, whole((EDGE, width + bc_width))),
            (edge_next, whole((EDGE, width + bc_width))),
            (step_raw, rows_back(LANES)),
            (step, rows_back(LANES)),
            (cumc, rows_back(LANES)),
            (cumd, rows_back(LANES)),
            (cumd, last_rows),
            (d_mixed, rows_back(width)),
            (d_values, rows_back(width)),
            (d_bc, rows_back(bc_width)),
            (d_step, rows_back(LANES)),
            (d_log, rows_back(LANES)),
            (conv_x, whole(conv_x.shape)),
            (conv_bc, whole(conv_bc.shape)),
            (small, small_spec),
            (col_out, whole((EDGE, width))),
        ],
        [
            ((tokens, width), bf16, rows_back(width)),
            ((tokens, half), bf16, rows_back(half)),
            ((tokens, half), f32, rows_back(half)),
            ((tokens, bc_width), bf16, rows_back(bc_width)),
            (
                (parts_head, bc_share + 2 * EDGE, tokens),
                f32,
                pl.BlockSpec(
                    (parts_head, bc_share + 2 * EDGE, CHUNK), lambda i: (0, 0, chunks - 1 - i)
                ),
            ),
            ((tokens, LANES), bf16, rows_back(LANES)),
            ((EDGE, model_width), f32, whole((EDGE, model_width))),
        ],
        [
            pltpu.VMEM((CHUNK + EDGE, width), f32),
            pltpu.VMEM((CHUNK + EDGE, bc_width), f32),
            pltpu.VMEM((CHUNK + EDGE, width), f32),
            pltpu.VMEM((CHUNK + EDGE, bc_width), f32),
        ],
    )
    peer = swap_cores(send)
    blocks = model_width // half
    per = ranges // blocks
    x_rows, small_rows = model_width // ranges, half // ranges
    bc_parts = lax.all_to_all(bc_rows, "head", 0, 0)
    shared = pl.BlockSpec((per, x_rows + small_rows, half), lambda i: (i, 0, 0))
    small_block = pl.BlockSpec((ranges, small_rows, half), lambda i: (0, x_rows // small_rows, 0))
    grad_x, gains_x = call(
        outer_kernel,
        blocks,
        [
            (core_flag, flag_spec),
            (normed, half_columns),
            (own, whole((tokens, half))),
            (normed_peer, half_columns),
            (peer, whole((tokens, half))),
            (w_x, rows_of(half, width)),
        ],
        [
            ((ranges, x_rows + small_rows, half), f32, shared),
            ((EDGE, model_width), f32, gain_block),
        ],
    )
    grad_x, bc_parts = lax.optimization_barrier((grad_x, bc_parts))
    grad_x = call(
        share_kernel,
        1,
        [
            (grad_x, pl.BlockSpec(memory_space=pl.ANY)),
            (bc_parts, whole(bc_parts.shape)),
            (step_low, whole(step_low.shape)),
            (normed, whole(normed.shape)),
            (sums, whole(sums.shape)),
            (gains_z, whole(gains_z.shape)),
            (gains_x, whole(gains_x.shape)),
            (norm_gain, whole((model_width,))),
            (bc_own_rows, whole(bc_own_rows.shape)),
            (dt_rows, whole(dt_rows.shape)),
        ],
        [(grad_x.shape, f32, small_block)],
        aliases={0: 0},
    )[0]

    grad_x, x_low = lax.optimization_barrier((grad_x, x_low))
    grad_x = lax.all_to_all(grad_x, "seq", 0, 0)
    features = 2 * LANES
    both, dots = call(
        norm_back_kernel,
        model_width // features,
        [
            (branch, pl.BlockSpec(memory_space=pl.ANY)),
            (gate_low, whole((tokens, width))),
            (x_low, whole((tokens, width))),
            (bc_low, whole((tokens, bc_width))),
            (step_low, whole((tokens, LANES))),
            (hid, whole((tokens, model_width))),
            (norm_gain, pl.BlockSpec((features,), lambda i: (i,))),
            (w_z, rows_of(features, width)),
            (w_x, rows_of(features, width)),
            (w_bc, rows_of(features, bc_width)),
            (dt_rows, pl.BlockSpec((heads_here, features), lambda i: (0, i))),
        ],
        [
            (
                (2, tokens, model_width),
                f32,
                pl.BlockSpec((1, tokens, features), lambda i: (1, 0, i)),
            ),
            ((EDGE, tokens), f32, whole((EDGE, tokens))),
        ],
        [pltpu.VMEM((tokens, LANES), f32), pltpu.VMEM((tokens, LANES), f32)],
        aliases={0: 0},
    )
    grad_x, both, dots = lax.optimization_barrier((grad_x, both, dots))
    lane_block = pl.BlockSpec(grad_x.shape[:2] + (LANES,), lambda i: (0, 0, i))
    grad_x = call(
        total_kernel, half // LANES, [(grad_x, lane_block)], [(grad_x.shape, f32, lane_block)]
    )[0]
    grad_x, both, dots = lax.optimization_barrier((grad_x, both, dots))
    grad_x = lax.all_to_all(grad_x, "seq", 0, 0)
    reduced = lax.psum_scatter(both, "head", scatter_dimension=2, tiled=True)
    row_dot = lax.psum(dots[0], "head")
    grad_x, row_dot, scale_in = lax.optimization_barrier((grad_x, row_dot, scale_in))
    x_peer = swap_cores(grad_x)
    grads = grad_x
    prefetched = functools.partial(
        pl.pallas_call,
        compiler_params=pltpu.CompilerParams(
            dimension_semantics=("arbitrary",), vmem_limit_bytes=58 * 2**20
        ),
        cost_estimate=pl.CostEstimate(flops=0, bytes_accessed=0, transcendentals=0),
    )
    block = pl.BlockSpec((per, x_rows + small_rows, half), lambda i, core: (i, 0, 0))
    half_of = pl.BlockSpec((half, half), lambda i, core: (i, core[0]))
    full = jax.ShapeDtypeStruct((model_width, width), f32)
    grad_x = prefetched(
        place_kernel,
        grid_spec=pltpu.PrefetchScalarGridSpec(
            num_scalar_prefetch=1, grid=(blocks,), in_specs=[block], out_specs=half_of
        ),
        out_shape=full,
    )(core_flag, grads)
    tiny_at = bc_share + 2 * EDGE + 7
    gains = grads.reshape(blocks, per, x_rows + small_rows, half)
    gains = gains[:, tiny_at // small_rows, x_rows + tiny_at % small_rows, :]
    gains = jnp.sum(lax.all_to_all(gains, "head", 0, 0), axis=0)
    g_norm = gains + swap_cores(gains)
    taps = conv_x.shape[0]
    shapes = [
        (bc_share, model_width),
        (heads_here, model_width),
        (taps, width),
        (taps, bc_width),
        (width,),
        (bc_width,),
        (width,),
        (heads_here,),
        (heads_here,),
        (heads_here,),
    ]

    def fixed(shape):
        return pl.BlockSpec(shape, lambda i, core: (0,) * len(shape))

    tiny_block = pl.BlockSpec(
        (ranges, small_rows, half), lambda i, core: (0, x_rows // small_rows, 0)
    )
    dealt = prefetched(
        deal_kernel,
        grid_spec=pltpu.PrefetchScalarGridSpec(
            num_scalar_prefetch=1,
            grid=(blocks,),
            in_specs=[block, tiny_block, tiny_block, pl.BlockSpec(memory_space=pl.ANY)],
            out_specs=[half_of] + [fixed(shape) for shape in shapes],
            scratch_shapes=[pltpu.VMEM((EDGE, model_width), f32)],
        ),
        out_shape=[full] + [jax.ShapeDtypeStruct(shape, f32) for shape in shapes],
        input_output_aliases={4: 0},
    )(1 - core_flag, x_peer, grads, x_peer, grad_x)
    grad_x, g_bc, g_dt, g_conv_x, g_conv_bc, g_bias_x, g_bias_bc, g_gain = dealt[:8]
    g_dt_bias, g_a_log, g_skip = dealt[8:]
    g_bc, grad_z, grad_out, g_norm = lax.optimization_barrier((g_bc, grad_z, grad_out, g_norm))
    reduced, grad_z, grad_out = lax.optimization_barrier((reduced, grad_z, grad_out))
    branch_own, norm_own = reduced[0], reduced[1]
    first = head_pos * share
    rows_own = lax.dynamic_slice_in_dim(hid, first, share, 1).astype(f32)
    output = (rows_own + branch_own).astype(bf16)[None]
    gain_own = lax.dynamic_slice_in_dim(norm_gain, first, share, 0)
    cot_own = lax.dynamic_slice_in_dim(cot, first, share, 1).astype(f32)
    unit_own = rows_own * scale_in
    grad_in = scale_in * (norm_own * gain_own - unit_own * row_dot[:, None] / model_width)
    hidden_grad = (cot_own + grad_in).astype(bf16)[None]
    return (
        output,
        hidden_grad,
        g_norm,
        grad_z,
        grad_x,
        g_bc.T,
        g_dt.T,
        g_conv_x,
        g_conv_bc,
        g_bias_x,
        g_bias_bc,
        g_dt_bias,
        g_a_log,
        g_skip,
        g_gain,
        grad_out,
    )


def solution(mesh):
    placed = (
        P("dp", "seq", None),
        P("dp", "seq", None),
        P(),
        P(None, "head"),
        P(None, "head"),
        P(),
        P(None, "head"),
        P(None, "head"),
        P(),
        P("head"),
        P(),
        P("head"),
        P("head"),
        P("head"),
        P("head"),
        P("head", None),
    )
    return jax.shard_map(
        per_device,
        mesh=mesh,
        in_specs=placed,
        out_specs=(
            P("dp", "seq", "head"),
            P("dp", "seq", "head"),
            P("head"),
            P(None, "head"),
            P(None, "head"),
            P(None, "head"),
            P(None, "head"),
            P(None, "head"),
            P(),
            P("head"),
            P(),
            P("head"),
            P("head"),
            P("head"),
            P("head"),
            P("head", None),
        ),
        check_vma=False,
    )
```
